256 devices in a mesh: rows: 64 (over x, y, z_lo, core), vec: 4 (over z_hi).
Axes of the slice: x: 4, y: 4, z: 8 (z_hi: 4, z_lo: 2; z = z_hi * 2 + z_lo), core: 2. Of those that a mesh axis runs over, the one named last changes fastest.
Arguments:
- walkers: bfloat16 [1024, 4800], P('rows'), may hold values from -6 to 6
- inv_intersection: bfloat16 [32, 150, 150], replicated, may hold values from -0.5 to 0.5
- rotated: bfloat16 [1024, 1024, 150], P('vec', 'rows'), may hold values from -0.875 to 0.875
- cholesky: bfloat16 [1024, 1024, 1024], P('vec', 'rows'), may hold values from -0.03125 to 0.03125
- field_noise: float32 [32, 1024], P(None, 'vec'), may hold values from -6 to 6
Outputs:
- fields: float32 [32, 1024], P(None, 'vec')
- propagated: bfloat16 [1024, 4800], P('rows', 'vec')
The draws below stay inside these ranges and needn't reach their ends.
All inputs are finite; a program needn't handle non-finite values.
Results may differ from the reference program's by a relative error of at most 0.014.
Values may be sent and summed in bfloat16 or wider, within the bound.
A program may use at most 128 MiB of HBM per device.

```python
import jax
import jax.numpy as jnp

NORB = 1024
NELEC = 150
NCHOL = 1024
WALKERS = 32
ORDER = 4


def level_of(stream_key, extent, split, least, high):
    level = 1.0
    for axis_at, shards_of in split:
        draws = jax.random.uniform(jax.random.fold_in(jax.random.fold_in(stream_key, 6), axis_at), (shards_of,), jnp.float32, least / len(split), high / len(split))
        level = level * jnp.repeat(jnp.exp(draws), extent[axis_at] // shards_of).reshape((-1,) + (1,) * (len(extent) - 1 - axis_at))
    return level


def bell_draw(own_key, extent, deviation, bound, pieces=(), held_as=jnp.bfloat16):
    array = jax.random.normal(own_key, extent, jnp.float32) * deviation
    if len(pieces) > 0:
        array = level_of(own_key, extent, pieces, -0.22, 0.18) * array
    return jnp.clip(array, min=-bound, max=bound).astype(held_as)


def setup_inputs(seed: int = 0) -> dict:
    key_of = jax.random.split(jax.random.key(seed), 6)
    return {
        "walkers": bell_draw(key_of[0], (NORB, WALKERS * NELEC), 1.0, 6.0, ((0, 64),)),
        "inv_intersection": bell_draw(key_of[1], (WALKERS, NELEC, NELEC), NELEC ** -0.5, 0.5),
        "rotated": bell_draw(key_of[2], (NCHOL, NORB, NELEC), 0.06, 0.875, ((0, 4), (1, 64))),
        "cholesky": bell_draw(key_of[3], (NCHOL, NORB, NORB), (NORB * NCHOL // 25) ** -0.5, 0.03125, ((0, 4), (1, 64))),
        "field_noise": bell_draw(key_of[4], (WALKERS, NCHOL), 1.0, 6.0, ((1, 4),), jnp.float32),
    }


time_root = 0.1


def reference(walkers, inv_intersection, rotated, cholesky, field_noise):
    stacked = walkers.reshape(NORB, WALKERS, NELEC)
    mixed_orbitals = jnp.einsum("pwf,wfe->pwe", stacked.astype(jnp.float32), inv_intersection.astype(jnp.float32)).astype(jnp.bfloat16)
    walker_major = jnp.transpose(mixed_orbitals, (1, 0, 2)).reshape(WALKERS, NORB * NELEC)
    force_bias = jnp.dot(walker_major, rotated.reshape(NCHOL, NORB * NELEC).T, preferred_element_type=jnp.float32)
    fields = field_noise - time_root * force_bias
    scaled = (-time_root * fields).astype(jnp.bfloat16)
    one_body = jnp.dot(scaled, cholesky.reshape(NCHOL, NORB * NORB), preferred_element_type=jnp.float32)
    one_body = one_body.astype(jnp.bfloat16).reshape(WALKERS, NORB, NORB)
    one_body_wide = one_body.astype(jnp.float32)
    taylor_term = stacked
    summed = stacked.astype(jnp.float32)
    for degree in range(1, ORDER + 1):
        product = jnp.einsum("wpq,qwe->pwe", one_body_wide, taylor_term.astype(jnp.float32))
        taylor_term = (product / degree).astype(jnp.bfloat16)
        summed = summed + taylor_term.astype(jnp.float32)
    return fields, summed.astype(jnp.bfloat16).reshape(NORB, WALKERS * NELEC)
```

```python
import functools

import jax
import jax.numpy as jnp
from jax import lax
from jax.experimental import pallas as pl
from jax.experimental.pallas import tpu as pltpu
from jax.sharding import PartitionSpec as P

MESH = pl.DeviceIdType.MESH
ORDER = 4
LANES = 128
TILE = 256

time_root = 0.1


def ceil_to(value, unit):
    return -(-value // unit) * unit


def kernel(
    dims,
    part_ref,
    noise_ref,
    phi_ref,
    chol_hbm,
    fields_ref,
    out_ref,
    chol,
    spread,
    wide,
    diag,
    fb_one,
    fb_two,
    fb_all,
    phi_block,
    terms,
    send_far,
    send_right,
    send_left,
    hold_right,
    hold_left,
    own,
    far_left,
    far_right,
    near_left,
    near_right,
    final,
    operator,
    result,
    landed,
    chol_sem,
    fb_send,
    fb_recv,
    phi_send,
    phi_recv,
    term_send,
    term_recv,
    far_send,
    far_recv,
    near_send,
    near_recv,
    op_send,
    op_recv,
    out_send,
    out_recv,
):
    na, nb, nh, rows, electrons = dims
    half = nb // 2
    block = nb * rows
    depth = chol.shape[0]
    orbitals = chol.shape[1]
    padded = terms.shape[1]
    r = lax.axis_index("rows")
    h = lax.axis_index("vec")
    a = r // nb
    b = r % nb

    def a_peer(i):
        return (((a + i) % na) * nb + b, h)

    def b_peer(i):
        return (a * nb + (b + i) % nb, h)

    def h_peer(i):
        return (r, (h + i) % nh)

    def send(src, dst, send_sem, recv_sem, peer):
        copy = pltpu.make_async_remote_copy(
            src_ref=src, dst_ref=dst, send_sem=send_sem, recv_sem=recv_sem, device_id=peer, device_id_type=MESH
        )
        copy.start()
        return copy

    def chunk(c):
        return (pl.ds(pl.multiple_of((c // 2) * 8, 8), 8), pl.ds(pl.multiple_of((c % 2) * LANES, LANES), LANES))

    load = pltpu.make_async_copy(chol_hbm, chol, chol_sem)
    load.start()

    barrier = pltpu.get_barrier_semaphore()
    peers = [a_peer(i) for i in range(1, na)] + [b_peer(i) for i in range(1, nb)] + [h_peer(1), h_peer(nh - 1)]
    for peer in peers:
        pl.semaphore_signal(barrier, inc=1, device_id=peer, device_id_type=MESH)
    pl.semaphore_wait(barrier, len(peers))

    sent = []

    copies = [
        send(part_ref.at[chunk((b + i) % nb)], fb_one.at[i], fb_send.at[0, i], fb_recv.at[0, i], b_peer(i))
        for i in range(1, nb)
    ]
    sent += copies
    phi_copies = [
        send(phi_ref.at[(b + i) % nb], phi_block.at[b], phi_send.at[i], phi_recv.at[i], b_peer(i)) for i in range(1, nb)
    ]
    sent += phi_copies
    phi_block[b] = phi_ref[b]

    def fill(k, _):
        row = lax.broadcasted_iota(jnp.int32, (spread.shape[0], TILE), 0)
        lane = lax.broadcasted_iota(jnp.int32, (spread.shape[0], TILE), 1)
        here = row == (TILE // rows) * k + lane // rows
        spread[:, pl.ds(pl.multiple_of(k * TILE, TILE), TILE)] = jnp.where(here, 1.0, 0.0).astype(jnp.bfloat16)
        return 0

    lax.fori_loop(0, depth // TILE, fill, 0)

    total = part_ref[chunk(b)]
    for i in range(1, nb):
        copies[i - 1].wait_recv()
        total = total + fb_one[i]
    fb_two[a] = total
    copies = [
        send(fb_two.at[a], fb_two.at[a], fb_send.at[1, i], fb_recv.at[1, i], a_peer(i)) for i in range(1, na)
    ]
    sent += copies
    for copy in copies:
        copy.wait_recv()
    total = fb_two[0]
    for i in range(1, na):
        total = total + fb_two[i]
    fb_all[chunk(b)] = total
    copies = [
        send(fb_all.at[chunk(b)], fb_all.at[chunk(b)], fb_send.at[2, i], fb_recv.at[2, i], b_peer(i))
        for i in range(1, nb)
    ]
    sent += copies

    for copy in phi_copies:
        copy.wait_recv()
    mine = pl.ds(pl.multiple_of(a * block, block), block)
    turned = jnp.transpose(phi_block[...].reshape(block, phi_block.shape[2]).astype(jnp.float32))
    first = turned[:padded, :]
    terms[0, :, mine] = first.astype(jnp.bfloat16)

    for copy in copies:
        copy.wait_recv()
    fields = noise_ref[...] - time_root * fb_all[...]
    fields_ref[...] = fields
    scaled = (-time_root * fields).astype(jnp.bfloat16)

    def share(k):
        return [
            send(terms.at[k, :, mine], terms.at[k, :, mine], term_send.at[k, i], term_recv.at[k, i], a_peer(i))
            for i in range(1, na)
        ]

    term_copies = share(0)
    sent += term_copies

    def widen(k, _):
        here = pl.ds(pl.multiple_of(k * TILE, TILE), TILE)
        wide[:, here] = jnp.dot(scaled, spread[:, here], preferred_element_type=jnp.float32)
        return 0

    lax.fori_loop(0, depth // TILE, widen, 0)
    load.wait()

    def multiply(c, store):
        def build(w, _):
            row = jnp.broadcast_to(wide[pl.ds(c * nb + w, 1), :], (rows, depth))
            p = lax.broadcasted_iota(jnp.int32, (rows, depth), 0)
            lane = lax.broadcasted_iota(jnp.int32, (rows, depth), 1)
            diag[pl.ds(pl.multiple_of(w * rows, rows), rows), :] = jnp.where(p == lane % rows, row, 0.0).astype(
                jnp.bfloat16
            )
            return 0

        lax.fori_loop(0, nb, build, 0)
        width = min(TILE, orbitals)

        def tile(n, _):
            here = pl.ds(pl.multiple_of(n * width, width), width)
            product = jnp.dot(diag[...], chol[:, here], preferred_element_type=jnp.float32)
            store(here, product.reshape(nb, rows, width))
            return 0

        lax.fori_loop(0, orbitals // width, tile, 0)

    def store_far(here, value):
        send_far[:, :, here] = value.astype(jnp.bfloat16)

    def store_right(here, value):
        hold_right[:, :, here] = value[:half]
        send_right[half:, :, here] = value[half:].astype(jnp.bfloat16)

    def store_left(here, value):
        send_left[:half, :, here] = value[:half].astype(jnp.bfloat16)
        hold_left[:, :, here] = value[half:]

    def store_own(here, value):
        own[:, :, here] = value

    lower, upper = pl.ds(0, half), pl.ds(half, half)
    multiply((h + 2) % nh, store_far)
    from_left = send(send_far.at[lower], far_left, far_send.at[0], far_recv.at[0], h_peer(1))
    from_right = send(send_far.at[upper], far_right, far_send.at[1], far_recv.at[1], h_peer(nh - 1))
    multiply((h + 1) % nh, store_right)
    early_left = send(send_right.at[upper], near_left.at[upper], near_send.at[0], near_recv.at[0], h_peer(1))
    multiply((h + nh - 1) % nh, store_left)
    early_right = send(send_left.at[lower], near_right.at[lower], near_send.at[1], near_recv.at[1], h_peer(nh - 1))
    sent += [from_left, from_right, early_left, early_right]
    multiply(h, store_own)

    late = [None] * nb
    from_left.wait_recv()
    from_right.wait_recv()
    for j in range(half):
        send_right[j] = (hold_right[j] + far_left[j].astype(jnp.float32)).astype(jnp.bfloat16)
        late[j] = send(send_right.at[j], near_left.at[j], near_send.at[2 + j], near_recv.at[2 + j], h_peer(1))
        k = half + j
        send_left[k] = (hold_left[j] + far_right[j].astype(jnp.float32)).astype(jnp.bfloat16)
        late[k] = send(send_left.at[k], near_right.at[k], near_send.at[2 + k], near_recv.at[2 + k], h_peer(nh - 1))
    sent += late
    early_left.wait_recv()
    early_right.wait_recv()

    def op_copy(j):
        return pltpu.make_async_remote_copy(
            src_ref=final.at[j],
            dst_ref=operator.at[b],
            send_sem=op_send.at[j],
            recv_sem=op_recv.at[b],
            device_id=(a * nb + j, h),
            device_id_type=MESH,
        )

    for j in [t * half + i for i in range(half) for t in range(2)]:
        late[j].wait_recv()
        value = own[j] + near_left[j].astype(jnp.float32) + near_right[j].astype(jnp.float32)
        final[j] = value.astype(jnp.bfloat16)

        @pl.when(j != b)
        def _():
            op_copy(j).start()

    operator[b] = final[b]
    for j in range(nb):

        @pl.when(j != b)
        def _():
            pltpu.make_async_remote_copy(
                src_ref=final.at[j],
                dst_ref=operator.at[j],
                send_sem=op_send.at[j],
                recv_sem=op_recv.at[j],
                device_id=(a * nb + j, h),
                device_id_type=MESH,
            ).wait_recv()

    summed = first
    for degree in range(1, ORDER + 1):
        for copy in term_copies:
            copy.wait_recv()
        product = lax.dot_general(
            terms[degree - 1],
            operator[...].reshape(block, orbitals),
            (((1,), (1,)), ((), ())),
            preferred_element_type=jnp.float32,
        )
        term = (product / degree).astype(jnp.bfloat16)
        summed = summed + term.astype(jnp.float32)
        if degree < ORDER:
            terms[degree, :, mine] = term
            term_copies = share(degree)
            sent += term_copies

    tall = jnp.concatenate([summed, jnp.zeros((result.shape[2] - padded, block), jnp.float32)], axis=0)
    result[...] = jnp.transpose(tall).astype(jnp.bfloat16).reshape(result.shape)
    copies = [
        send(result.at[(b + i) % nb], landed.at[b], out_send.at[i], out_recv.at[i], b_peer(i)) for i in range(1, nb)
    ]
    sent += copies
    landed[b] = result[b]
    for copy in copies:
        copy.wait_recv()
    out_ref[...] = landed[...]

    for copy in sent:
        copy.wait_send()
    for j in range(nb):

        @pl.when(j != b)
        def _():
            op_copy(j).wait_send()


def local(na, nb, nh, walkers, inv_intersection, rotated, cholesky, field_noise):
    walker_count, electrons = inv_intersection.shape[:2]
    rows = walkers.shape[0]
    vectors, _, orbitals = cholesky.shape
    stacked = walkers.reshape(rows, walker_count, electrons)
    mixed_orbitals = jnp.einsum(
        "pwf,wfe->pwe", stacked, inv_intersection, preferred_element_type=jnp.float32
    ).astype(jnp.bfloat16)
    partial_value = jnp.einsum("pwe,gpe->wg", mixed_orbitals, rotated, preferred_element_type=jnp.float32)

    wide_electrons = ceil_to(electrons, LANES)
    padded = ceil_to(electrons, 16)
    block = lax.dynamic_slice_in_dim(walkers, lax.axis_index("vec") * (nb * electrons), nb * electrons, 1)
    block = jnp.transpose(block.reshape(rows, nb, electrons), (1, 0, 2))
    block = jnp.pad(block, ((0, 0), (0, 0), (0, wide_electrons - electrons)))

    half = nb // 2
    bf16, f32 = jnp.bfloat16, jnp.float32
    depth = vectors * rows
    dma = pltpu.SemaphoreType.DMA
    vmem = pl.BlockSpec(memory_space=pltpu.VMEM)
    piece = (nb, rows, orbitals)
    fields, out = pl.pallas_call(
        functools.partial(kernel, (na, nb, nh, rows, electrons)),
        out_shape=(
            jax.ShapeDtypeStruct((walker_count, vectors), f32),
            jax.ShapeDtypeStruct((nb, rows, wide_electrons), bf16),
        ),
        in_specs=[vmem, vmem, vmem, pl.BlockSpec(memory_space=pl.ANY)],
        out_specs=(vmem, vmem),
        scratch_shapes=[
            pltpu.VMEM((depth, orbitals), bf16),
            pltpu.VMEM((vectors, depth), bf16),
            pltpu.VMEM((walker_count, depth), f32),
            pltpu.VMEM((nb * rows, depth), bf16),
            pltpu.VMEM((nb, 8, LANES), f32),
            pltpu.VMEM((na, 8, LANES), f32),
            pltpu.VMEM((walker_count, vectors), f32),
            pltpu.VMEM((nb, rows, wide_electrons), bf16),
            pltpu.VMEM((ORDER, padded, orbitals), bf16),
            pltpu.VMEM(piece, bf16),
            pltpu.VMEM(piece, bf16),
            pltpu.VMEM(piece, bf16),
            pltpu.VMEM((half, rows, orbitals), f32),
            pltpu.VMEM((half, rows, orbitals), f32),
            pltpu.VMEM(piece, f32),
            pltpu.VMEM((half, rows, orbitals), bf16),
            pltpu.VMEM((half, rows, orbitals), bf16),
            pltpu.VMEM(piece, bf16),
            pltpu.VMEM(piece, bf16),
            pltpu.VMEM(piece, bf16),
            pltpu.VMEM(piece, bf16),
            pltpu.VMEM((nb, rows, wide_electrons), bf16),
            pltpu.VMEM((nb, rows, wide_electrons), bf16),
            dma,
            dma((3, 8)),
            dma((3, 8)),
            dma((nb,)),
            dma((nb,)),
            dma((ORDER, na)),
            dma((ORDER, na)),
            dma((2,)),
            dma((2,)),
            dma((nb + 2,)),
            dma((nb + 2,)),
            dma((nb,)),
            dma((nb,)),
            dma((nb,)),
            dma((nb,)),
        ],
        compiler_params=pltpu.CompilerParams(
            collective_id=0, has_side_effects=True, vmem_limit_bytes=48 * 1024 * 1024
        ),
    )(partial_value, field_noise, block, cholesky.reshape(depth, orbitals))
    propagated = jnp.transpose(out[:, :, :electrons], (1, 0, 2)).reshape(rows, nb * electrons)
    return fields, propagated


def solution(mesh):
    nh = mesh.shape["vec"]
    nb = 8 if mesh.shape["rows"] == 64 else 2
    na = mesh.shape["rows"] // nb
    placed = (P("rows", None), P(), P("vec", "rows", None), P("vec", "rows", None), P(None, "vec"))
    return jax.shard_map(
        functools.partial(local, na, nb, nh),
        mesh=mesh,
        in_specs=placed,
        out_specs=(P(None, "vec"), P("rows", "vec")),
        check_vma=False,
    )
```

```python
import functools

import jax
import jax.numpy as jnp
from jax import lax
from jax.experimental import pallas as pl
from jax.experimental.pallas import tpu as pltpu
from jax.sharding import PartitionSpec as P

MESH = pl.DeviceIdType.MESH
ORDER = 4
LANES = 128
TILE = 256
PARTS = 2

time_root = 0.1


def ceil_to(value, unit):
    return -(-value // unit) * unit


def place(nb, r):
    if nb == 2:
        return r % 2, r // 2
    x, y, low = r // 16, (r // 4) % 4, r % 4
    return ((y + y // 2) % 2) * 4 + low, x * 2 + y // 2


def device(nb, a, b):
    if nb == 2:
        return b * 2 + a
    x, half = b // 2, b % 2
    return x * 16 + (2 * half + (a // 4 + half) % 2) * 4 + a % 4


def kernel(
    dims,
    walkers_hbm,
    inverse_hbm,
    rotated_hbm,
    chol_hbm,
    noise_ref,
    fields_ref,
    out_ref,
    walkers,
    inverse,
    rotated,
    chol,
    wide_low,
    wide_high,
    mixed,
    mixed_diag,
    part,
    phi,
    spread,
    order,
    wide,
    diag,
    fb_one,
    fb_two,
    fb_all,
    phi_block,
    terms,
    send_far,
    send_right,
    send_left,
    hold_right,
    hold_left,
    own,
    far_left,
    far_right,
    near_left,
    near_right,
    final,
    operator,
    turned_operator,
    result,
    landed,
    load_sem,
    fb_send,
    fb_recv,
    phi_send,
    phi_recv,
    term_send,
    term_recv,
    far_send,
    far_recv,
    near_send,
    near_recv,
    late_send,
    late_recv,
    op_send,
    op_recv,
    out_send,
    out_recv,
):
    na, nb, nh, rows, electrons = dims
    half = nb // 2
    block = nb * rows
    depth = chol.shape[0]
    orbitals = chol.shape[1]
    padded = terms.shape[1]
    r = lax.axis_index("rows")
    h = lax.axis_index("vec")
    a, b = place(nb, r)

    def a_peer(i):
        return (device(nb, (a + i) % na, b), h)

    def b_peer(i):
        return (device(nb, a, (b + i) % nb), h)

    def h_peer(i):
        return (r, (h + i) % nh)

    def send(src, dst, send_sem, recv_sem, peer):
        copy = pltpu.make_async_remote_copy(
            src_ref=src, dst_ref=dst, send_sem=send_sem, recv_sem=recv_sem, device_id=peer, device_id_type=MESH
        )
        copy.start()
        return copy

    def chunk(c):
        return (pl.ds(pl.multiple_of((c // 2) * 8, 8), 8), pl.ds(pl.multiple_of((c % 2) * LANES, LANES), LANES))

    pairs = ((walkers_hbm, walkers), (inverse_hbm, inverse), (rotated_hbm, rotated), (chol_hbm, chol))
    loads = [pltpu.make_async_copy(src, dst, load_sem.at[i]) for i, (src, dst) in enumerate(pairs)]
    for load in loads:
        load.start()

    barrier = pltpu.get_barrier_semaphore()
    peers = [a_peer(i) for i in range(1, na)] + [b_peer(i) for i in range(1, nb)] + [h_peer(1), h_peer(nh - 1)]
    for peer in peers:
        pl.semaphore_signal(barrier, inc=1, device_id=peer, device_id_type=MESH)
    def fill(k, _):
        row = lax.broadcasted_iota(jnp.int32, (spread.shape[0], TILE), 0)
        lane = lax.broadcasted_iota(jnp.int32, (spread.shape[0], TILE), 1)
        here = row == (TILE // rows) * k + lane // rows
        spread[:, pl.ds(pl.multiple_of(k * TILE, TILE), TILE)] = jnp.where(here, 1.0, 0.0).astype(jnp.bfloat16)
        return 0

    lax.fori_loop(0, depth // TILE, fill, 0)

    count = mixed.shape[0]
    span = electrons * rows
    loads[1].wait()
    wide_low[: electrons * count, :] = inverse[:, :, :LANES].astype(jnp.float32).reshape(electrons * count, LANES)
    wide_high[: electrons * count, : electrons - LANES] = (
        inverse[:, :, LANES:].astype(jnp.float32).reshape(electrons * count, electrons - LANES)
    )
    loads[0].wait()
    for w in range(count):
        low = wide_low[pl.ds(w, ceil_to(electrons, 8), stride=count), :]
        high = wide_high[pl.ds(w, ceil_to(electrons, 8), stride=count), :]
        matrix = jnp.concatenate([low, high], axis=1).astype(jnp.bfloat16)[:electrons, :electrons]
        mixed[w] = jnp.dot(
            walkers[:, w * electrons : (w + 1) * electrons], matrix, preferred_element_type=jnp.float32
        ).astype(jnp.bfloat16)
    spaced = jnp.dot(
        mixed[...].reshape(count * rows, electrons), spread[:electrons, :span], preferred_element_type=jnp.float32
    )
    p = lax.broadcasted_iota(jnp.int32, spaced.shape, 0) % rows
    lane = lax.broadcasted_iota(jnp.int32, spaced.shape, 1) % rows
    mixed_diag[...] = jnp.where(p == lane, spaced, 0.0).astype(jnp.bfloat16)
    loads[2].wait()
    by_row = jnp.dot(mixed_diag[...], rotated[...], preferred_element_type=jnp.float32)
    part[...] = jnp.sum(by_row.reshape(count, rows, by_row.shape[1]), axis=1)

    phi[:, :, LANES:] = jnp.zeros((nb, rows, phi.shape[2] - LANES), jnp.bfloat16)
    for k in range(nh):

        @pl.when(h == k)
        def _():
            for j in range(nb):
                start = (k * nb + j) * electrons
                phi[j, :, :electrons] = walkers[:, start : start + electrons]

    pl.semaphore_wait(barrier, len(peers))

    sent = []

    copies = [
        send(part.at[chunk((a + i) % na)], fb_one.at[i], fb_send.at[0, i], fb_recv.at[0, i], a_peer(i))
        for i in range(1, na)
    ]
    sent += copies

    def arrange(k, _):
        lane = lax.broadcasted_iota(jnp.int32, (1, block), 1)
        source = device(nb, k, lane // rows) * rows + lane % rows
        row = lax.broadcasted_iota(jnp.int32, (orbitals, block), 0)
        here = pl.ds(pl.multiple_of(k * block, block), block)
        order[:, here] = jnp.where(row == source, 1.0, 0.0).astype(jnp.bfloat16)
        return 0

    lax.fori_loop(0, na, arrange, 0)

    total = part[chunk(a)]
    for i in range(1, na):
        copies[i - 1].wait_recv()
        total = total + fb_one[i]
    fb_two[b] = total
    copies = [
        send(fb_two.at[b], fb_two.at[b], fb_send.at[1, i], fb_recv.at[1, i], b_peer(i)) for i in range(1, nb)
    ]
    sent += copies
    phi_copies = [
        send(phi.at[(b + i) % nb], phi_block.at[b], phi_send.at[i], phi_recv.at[i], b_peer(i)) for i in range(1, nb)
    ]
    sent += phi_copies
    phi_block[b] = phi[b]
    for copy in copies:
        copy.wait_recv()
    total = fb_two[0]
    for i in range(1, nb):
        total = total + fb_two[i]
    fb_all[chunk(a)] = total
    copies = [
        send(fb_all.at[chunk(a)], fb_all.at[chunk(a)], fb_send.at[2, i], fb_recv.at[2, i], a_peer(i))
        for i in range(1, na)
    ]
    sent += copies

    for copy in phi_copies:
        copy.wait_recv()
    mine = pl.ds(pl.multiple_of(a * block, block), block)
    turned = jnp.transpose(phi_block[...].reshape(block, phi_block.shape[2]).astype(jnp.float32))
    first = turned[:padded, :]
    terms[0, :, mine] = first.astype(jnp.bfloat16)

    for copy in copies:
        copy.wait_recv()
    fields = noise_ref[...] - time_root * fb_all[...]
    fields_ref[...] = fields
    scaled = (-time_root * fields).astype(jnp.bfloat16)

    def some(c):
        return pl.ds(c * (padded // PARTS), padded // PARTS)

    def share(k, c):
        there = terms.at[k, some(c), mine]
        return [send(there, there, term_send.at[k, c, i], term_recv.at[k, c, i], a_peer(i)) for i in range(1, na)]

    term_copies = [share(0, c) for c in range(PARTS)]
    sent += sum(term_copies, [])

    wide[...] = jnp.dot(scaled, spread[...], preferred_element_type=jnp.float32)
    loads[3].wait()

    lower, upper = pl.ds(0, half), pl.ds(half, half)
    width = min(TILE, orbitals)
    tiles = orbitals // width

    def multiply(c, store):
        def build(w, _):
            row = jnp.broadcast_to(wide[pl.ds(c * nb + w, 1), :], (rows, depth))
            p = lax.broadcasted_iota(jnp.int32, (rows, depth), 0)
            lane = lax.broadcasted_iota(jnp.int32, (rows, depth), 1)
            diag[pl.ds(pl.multiple_of(w * rows, rows), rows), :] = jnp.where(p == lane % rows, row, 0.0).astype(
                jnp.bfloat16
            )
            return 0

        lax.fori_loop(0, nb, build, 0)
        for n in range(tiles):
            here = pl.ds(n * width, width)
            product = jnp.dot(diag[...], chol[:, here], preferred_element_type=jnp.float32)
            store(n, here, product.reshape(nb, rows, width))

    from_left, from_right, early_left, early_right = [], [], [], []

    def store_far(n, here, value):
        send_far[:, :, here] = value.astype(jnp.bfloat16)
        src = send_far.at[lower, :, here]
        from_left.append(send(src, far_left.at[:, :, here], far_send.at[0, n], far_recv.at[0, n], h_peer(1)))
        src = send_far.at[upper, :, here]
        from_right.append(send(src, far_right.at[:, :, here], far_send.at[1, n], far_recv.at[1, n], h_peer(nh - 1)))

    def store_right(n, here, value):
        hold_right[:, :, here] = value[:half]
        send_right[half:, :, here] = value[half:].astype(jnp.bfloat16)
        there = (upper, slice(None), here)
        early_left.append(
            send(send_right.at[there], near_left.at[there], near_send.at[0, n], near_recv.at[0, n], h_peer(1))
        )

    def store_left(n, here, value):
        send_left[:half, :, here] = value[:half].astype(jnp.bfloat16)
        hold_left[:, :, here] = value[half:]
        there = (lower, slice(None), here)
        early_right.append(
            send(send_left.at[there], near_right.at[there], near_send.at[1, n], near_recv.at[1, n], h_peer(nh - 1))
        )

    def store_own(n, here, value):
        own[:, :, here] = value

    multiply((h + 2) % nh, store_far)
    multiply((h + 1) % nh, store_right)
    multiply((h + nh - 1) % nh, store_left)
    multiply(h, store_own)
    sent += from_left + from_right + early_left + early_right

    late, op_copies = [], []
    for n in range(tiles):
        here = pl.ds(n * width, width)
        from_left[n].wait_recv()
        send_right[:half, :, here] = (hold_right[:, :, here] + far_left[:, :, here].astype(jnp.float32)).astype(
            jnp.bfloat16
        )
        there = (lower, slice(None), here)
        late.append(
            send(send_right.at[there], near_left.at[there], late_send.at[0, n], late_recv.at[0, n], h_peer(1))
        )
        from_right[n].wait_recv()
        send_left[half:, :, here] = (hold_left[:, :, here] + far_right[:, :, here].astype(jnp.float32)).astype(
            jnp.bfloat16
        )
        there = (upper, slice(None), here)
        late.append(
            send(send_left.at[there], near_right.at[there], late_send.at[1, n], late_recv.at[1, n], h_peer(nh - 1))
        )
    sent += late
    for n in range(tiles):
        here = pl.ds(n * width, width)
        for copy in (early_left[n], early_right[n], late[2 * n], late[2 * n + 1]):
            copy.wait_recv()
        value = own[:, :, here] + near_left[:, :, here].astype(jnp.float32) + near_right[:, :, here].astype(jnp.float32)
        final[:, :, here] = value.astype(jnp.bfloat16)
        op_copies += [
            send(
                final.at[(b + i) % nb, :, here],
                operator.at[b, :, here],
                op_send.at[n, i],
                op_recv.at[n, i],
                b_peer(i),
            )
            for i in range(1, nb)
        ]
    sent += op_copies
    operator[b] = final[b]
    for copy in op_copies:
        copy.wait_recv()

    turned_operator[...] = jnp.dot(
        operator[...].reshape(block, orbitals), order[...], preferred_element_type=jnp.float32
    ).astype(jnp.bfloat16)
    summed = [first[c * (padded // PARTS) : (c + 1) * (padded // PARTS)] for c in range(PARTS)]
    for degree in range(1, ORDER + 1):
        for c in range(PARTS):
            for copy in term_copies[c]:
                copy.wait_recv()
            product = lax.dot_general(
                terms[degree - 1, some(c), :],
                turned_operator[...],
                (((1,), (1,)), ((), ())),
                preferred_element_type=jnp.float32,
            )
            term = (product / degree).astype(jnp.bfloat16)
            if degree < ORDER:
                terms[degree, some(c), mine] = term
                term_copies[c] = share(degree, c)
                sent += term_copies[c]
            summed[c] = summed[c] + term.astype(jnp.float32)

    tall = jnp.concatenate([*summed, jnp.zeros((result.shape[2] - padded, block), jnp.float32)], axis=0)
    result[...] = jnp.transpose(tall).astype(jnp.bfloat16).reshape(result.shape)
    copies = [
        send(result.at[(b + i) % nb], landed.at[b], out_send.at[i], out_recv.at[i], b_peer(i)) for i in range(1, nb)
    ]
    sent += copies
    landed[b] = result[b]
    for copy in copies:
        copy.wait_recv()
    for j in range(nb):
        out_ref[:, j * electrons : (j + 1) * electrons] = landed[j, :, :electrons]

    for copy in sent:
        copy.wait_send()


def local(na, nb, nh, walkers, inv_intersection, rotated, cholesky, field_noise):
    walker_count, electrons = inv_intersection.shape[:2]
    rows = walkers.shape[0]
    vectors, _, orbitals = cholesky.shape
    wide_electrons = ceil_to(electrons, LANES)
    padded = ceil_to(electrons, 16)
    half = nb // 2
    bf16, f32 = jnp.bfloat16, jnp.float32
    depth = vectors * rows
    dma = pltpu.SemaphoreType.DMA
    vmem = pl.BlockSpec(memory_space=pltpu.VMEM)
    piece = (nb, rows, orbitals)
    fields, propagated = pl.pallas_call(
        functools.partial(kernel, (na, nb, nh, rows, electrons)),
        out_shape=(
            jax.ShapeDtypeStruct((walker_count, vectors), f32),
            jax.ShapeDtypeStruct((rows, nb * electrons), bf16),
        ),
        in_specs=[pl.BlockSpec(memory_space=pl.ANY)] * 4 + [vmem],
        out_specs=(vmem, vmem),
        scratch_shapes=[
            pltpu.VMEM(walkers.shape, bf16),
            pltpu.VMEM((electrons, walker_count, electrons), bf16),
            pltpu.VMEM((electrons * rows, vectors), bf16),
            pltpu.VMEM((depth, orbitals), bf16),
            pltpu.VMEM((ceil_to(electrons, 8) * walker_count, LANES), f32),
            pltpu.VMEM((ceil_to(electrons, 8) * walker_count, LANES), f32),
            pltpu.VMEM((walker_count, rows, electrons), bf16),
            pltpu.VMEM((walker_count * rows, electrons * rows), bf16),
            pltpu.VMEM((walker_count, vectors), f32),
            pltpu.VMEM((nb, rows, wide_electrons), bf16),
            pltpu.VMEM((vectors, depth), bf16),
            pltpu.VMEM((orbitals, orbitals), bf16),
            pltpu.VMEM((walker_count, depth), f32),
            pltpu.VMEM((nb * rows, depth), bf16),
            pltpu.VMEM((na, 8, LANES), f32),
            pltpu.VMEM((nb, 8, LANES), f32),
            pltpu.VMEM((walker_count, vectors), f32),
            pltpu.VMEM((nb, rows, wide_electrons), bf16),
            pltpu.VMEM((ORDER, padded, orbitals), bf16),
            pltpu.VMEM(piece, bf16),
            pltpu.VMEM(piece, bf16),
            pltpu.VMEM(piece, bf16),
            pltpu.VMEM((half, rows, orbitals), f32),
            pltpu.VMEM((half, rows, orbitals), f32),
            pltpu.VMEM(piece, f32),
            pltpu.VMEM((half, rows, orbitals), bf16),
            pltpu.VMEM((half, rows, orbitals), bf16),
            pltpu.VMEM(piece, bf16),
            pltpu.VMEM(piece, bf16),
            pltpu.VMEM(piece, bf16),
            pltpu.VMEM(piece, bf16),
            pltpu.VMEM((nb * rows, orbitals), bf16),
            pltpu.VMEM((nb, rows, wide_electrons), bf16),
            pltpu.VMEM((nb, rows, wide_electrons), bf16),
            dma((4,)),
            dma((3, 8)),
            dma((3, 8)),
            dma((nb,)),
            dma((nb,)),
            dma((ORDER, PARTS, na)),
            dma((ORDER, PARTS, na)),
            dma((2, 4)),
            dma((2, 4)),
            dma((2, 4)),
            dma((2, 4)),
            dma((2, 4)),
            dma((2, 4)),
            dma((4, nb)),
            dma((4, nb)),
            dma((nb,)),
            dma((nb,)),
        ],
        compiler_params=pltpu.CompilerParams(
            collective_id=0, has_side_effects=True, vmem_limit_bytes=62 * 1024 * 1024
        ),
    )(
        walkers,
        jnp.transpose(inv_intersection, (1, 0, 2)),
        jnp.transpose(rotated, (2, 1, 0)).reshape(electrons * rows, vectors),
        cholesky.reshape(depth, orbitals),
        field_noise,
    )
    return fields, propagated


def solution(mesh):
    nh = mesh.shape["vec"]
    nb = 8 if mesh.shape["rows"] == 64 else 2
    na = mesh.shape["rows"] // nb
    placed = (P("rows", None), P(), P("vec", "rows", None), P("vec", "rows", None), P(None, "vec"))
    return jax.shard_map(
        functools.partial(local, na, nb, nh),
        mesh=mesh,
        in_specs=placed,
        out_specs=(P(None, "vec"), P("rows", "vec")),
        check_vma=False,
    )
```

```python
import functools

import jax
import jax.numpy as jnp
from jax import lax
from jax.experimental import pallas as pl
from jax.experimental.pallas import tpu as pltpu
from jax.sharding import PartitionSpec as P

MESH = pl.DeviceIdType.MESH
ORDER = 4
LANES = 128
TILE = 256
PARTS = 5

time_root = 0.1


def ceil_to(value, unit):
    return -(-value // unit) * unit


def place(nb, r):
    if nb == 2:
        return r % 2, r // 2
    x, y, low = r // 16, (r // 4) % 4, r % 4
    return ((y + y // 2) % 2) * 4 + low, x * 2 + y // 2


def device(nb, a, b):
    if nb == 2:
        return b * 2 + a
    x, half = b // 2, b % 2
    return x * 16 + (2 * half + (a // 4 + half) % 2) * 4 + a % 4


def kernel(
    dims,
    walkers_hbm,
    inverse_hbm,
    rotated_hbm,
    chol_hbm,
    noise_hbm,
    fields_ref,
    out_ref,
    walkers,
    inverse,
    rotated,
    chol,
    noise,
    wide_low,
    wide_high,
    mixed,
    mixed_diag,
    part,
    phi,
    spread,
    order,
    wide,
    diag,
    fb_one,
    fb_two,
    fb_all,
    phi_block,
    terms,
    send_far,
    send_right,
    send_left,
    hold_right,
    hold_left,
    own,
    far_left,
    far_right,
    near_left,
    near_right,
    final,
    operator,
    turned_operator,
    result,
    landed,
    load_sem,
    fb_send,
    fb_recv,
    phi_sem,
    term_send,
    term_recv,
    far_send,
    far_recv,
    near_send,
    near_recv,
    late_send,
    late_recv,
    op_send,
    op_recv,
    out_sem,
):
    na, nb, nh, rows, electrons = dims
    half = nb // 2
    block = nb * rows
    depth = chol.shape[0]
    orbitals = chol.shape[1]
    padded = terms.shape[1]
    r = lax.axis_index("rows")
    h = lax.axis_index("vec")
    a, b = place(nb, r)

    def a_at(i):
        return sum(((a // bit) % 2 if not (na - i) // bit % 2 else 1 - (a // bit) % 2) * bit for bit in (4, 2, 1) if bit < na)

    def b_at(i):
        if nb == 2:
            return 1 - b
        step, turn = ((2, 1), (1, 1), (3, 1), (2, 0), (1, 0), (3, 0), (0, 1))[i - 1]
        return (b // 2 + step) % 4 * 2 + (1 - b % 2 if turn else b % 2)

    def a_peer(i):
        return (device(nb, a_at(i), b), h)

    def b_peer(i):
        return (device(nb, a, b_at(i)), h)

    def h_peer(i):
        return (r, (h + i) % nh)

    def send(src, dst, send_sem, recv_sem, peer):
        copy = pltpu.make_async_remote_copy(
            src_ref=src, dst_ref=dst, send_sem=send_sem, recv_sem=recv_sem, device_id=peer, device_id_type=MESH
        )
        copy.start()

    def wait(span, sem):
        pltpu.make_async_copy(span, span, sem).wait()

    def chunk(c):
        return (pl.ds(pl.multiple_of((c // 2) * 8, 8), 8), pl.ds(pl.multiple_of((c % 2) * LANES, LANES), LANES))

    pairs = ((walkers_hbm, walkers), (inverse_hbm, inverse), (rotated_hbm, rotated), (chol_hbm, chol), (noise_hbm, noise))
    loads = [pltpu.make_async_copy(src, dst, load_sem.at[i]) for i, (src, dst) in enumerate(pairs)]
    for load in loads:
        load.start()

    barrier = pltpu.get_barrier_semaphore()
    peers = [a_peer(i) for i in range(1, na)] + [b_peer(i) for i in range(1, nb)] + [h_peer(1), h_peer(nh - 1)]
    for peer in peers:
        pl.semaphore_signal(barrier, inc=1, device_id=peer, device_id_type=MESH)
    def fill(k, _):
        row = lax.broadcasted_iota(jnp.int32, (spread.shape[0], TILE), 0)
        lane = lax.broadcasted_iota(jnp.int32, (spread.shape[0], TILE), 1)
        here = row == (TILE // rows) * k + lane // rows
        spread[:, pl.ds(pl.multiple_of(k * TILE, TILE), TILE)] = jnp.where(here, 1.0, 0.0).astype(jnp.bfloat16)
        return 0

    lax.fori_loop(0, depth // TILE, fill, 0)

    count = mixed.shape[0]
    span = electrons * rows
    loads[1].wait()
    wide_low[: electrons * count, :] = inverse[:, :, :LANES].astype(jnp.float32).reshape(electrons * count, LANES)
    wide_high[: electrons * count, : electrons - LANES] = (
        inverse[:, :, LANES:].astype(jnp.float32).reshape(electrons * count, electrons - LANES)
    )
    loads[0].wait()
    for w in range(count):
        low = wide_low[pl.ds(w, ceil_to(electrons, 8), stride=count), :]
        high = wide_high[pl.ds(w, ceil_to(electrons, 8), stride=count), :]
        matrix = jnp.concatenate([low, high], axis=1).astype(jnp.bfloat16)[:electrons, :electrons]
        mixed[w] = jnp.dot(
            walkers[:, w * electrons : (w + 1) * electrons], matrix, preferred_element_type=jnp.float32
        ).astype(jnp.bfloat16)
    for start in range(0, span, TILE):
        here = pl.ds(start, min(TILE, span - start))
        spaced = jnp.dot(
            mixed[...].reshape(count * rows, electrons), spread[:electrons, here], preferred_element_type=jnp.float32
        )
        p = lax.broadcasted_iota(jnp.int32, spaced.shape, 0) % rows
        lane = lax.broadcasted_iota(jnp.int32, spaced.shape, 1) % rows
        mixed_diag[:, here] = jnp.where(p == lane, spaced, 0.0).astype(jnp.bfloat16)
    phi[:, :, LANES:] = jnp.zeros((nb, rows, phi.shape[2] - LANES), jnp.bfloat16)
    for k in range(nh):

        @pl.when(h == k)
        def _():
            for j in range(nb):
                start = (k * nb + j) * electrons
                phi[j, :, :electrons] = walkers[:, start : start + electrons]

    pl.semaphore_wait(barrier, len(peers))

    for i in range(1, nb):
        send(phi.at[b_at(i)], phi_block.at[b], phi_sem.at[0], phi_sem.at[1], b_peer(i))
    phi_block[b] = phi[b]
    loads[2].wait()
    by_row = jnp.dot(mixed_diag[...], rotated[...], preferred_element_type=jnp.float32)
    part[...] = jnp.sum(by_row.reshape(count, rows, by_row.shape[1]), axis=1)

    for i in range(1, na):
        send(part.at[chunk(a_at(i))], fb_one.at[i], fb_send.at[0], fb_recv.at[0], a_peer(i))

    def arrange(k, _):
        lane = lax.broadcasted_iota(jnp.int32, (1, block), 1)
        source = device(nb, k, lane // rows) * rows + lane % rows
        row = lax.broadcasted_iota(jnp.int32, (orbitals, block), 0)
        here = pl.ds(pl.multiple_of(k * block, block), block)
        order[:, here] = jnp.where(row == source, 1.0, 0.0).astype(jnp.bfloat16)
        return 0

    lax.fori_loop(0, na, arrange, 0)

    fb_chunks = fb_one.at[pl.ds(1, na - 1)]
    wait(fb_chunks, fb_recv.at[0])
    total = part[chunk(a)]
    for i in range(1, na):
        total = total + fb_one[i]
    fb_two[b] = total
    for i in range(1, nb):
        send(fb_two.at[b], fb_two.at[b], fb_send.at[1], fb_recv.at[1], b_peer(i))

    wait(phi_block.at[pl.ds(0, nb - 1)], phi_sem.at[1])
    mine = pl.ds(pl.multiple_of(a * block, block), block)
    turned = jnp.transpose(phi_block[...].reshape(block, phi_block.shape[2]).astype(jnp.float32))
    first = turned[:padded, :]
    terms[0, :, mine] = first.astype(jnp.bfloat16)

    def some(c):
        return pl.ds(c * (padded // PARTS), padded // PARTS)

    def share(k, c):
        there = terms.at[k, some(c), mine]
        for i in range(1, na):
            send(there, there, term_send.at[k], term_recv.at[k, c], a_peer(i))

    for c in range(PARTS):
        share(0, c)

    wait(fb_two.at[pl.ds(0, nb - 1)], fb_recv.at[1])
    total = fb_two[0]
    for i in range(1, nb):
        total = total + fb_two[i]
    fb_all[chunk(a)] = total
    for i in range(1, na):
        send(fb_all.at[chunk(a)], fb_all.at[chunk(a)], fb_send.at[2], fb_recv.at[2], a_peer(i))

    wait(fb_chunks, fb_recv.at[2])
    loads[4].wait()
    fields = noise[...] - time_root * fb_all[...]
    fields_ref[...] = fields
    scaled = (-time_root * fields).astype(jnp.bfloat16)

    wide[...] = jnp.dot(scaled, spread[...], preferred_element_type=jnp.float32)
    loads[3].wait()

    lower, upper = pl.ds(0, half), pl.ds(half, half)
    width = min(TILE, orbitals)
    tiles = orbitals // width

    def build(slot, c):
        p = lax.broadcasted_iota(jnp.int32, (rows, depth), 0)
        lane = lax.broadcasted_iota(jnp.int32, (rows, depth), 1)
        for w in range(nb):
            row = jnp.broadcast_to(wide[pl.ds(c * nb + w, 1), :], (rows, depth))
            diag[slot, w * rows : (w + 1) * rows, :] = jnp.where(p == lane % rows, row, 0.0).astype(jnp.bfloat16)

    def multiply(slot, store, some_spots):
        for here in some_spots:
            product = jnp.dot(diag[slot], chol[:, here], preferred_element_type=jnp.float32)
            store(here, product.reshape(nb, rows, width))

    def store_far(here, value):
        send_far[:, :, here] = value.astype(jnp.bfloat16)

    def store_right(here, value):
        hold_right[:, :, here] = value[:half]
        send_right[half:, :, here] = value[half:].astype(jnp.bfloat16)

    def store_left(here, value):
        send_left[:half, :, here] = value[:half].astype(jnp.bfloat16)
        hold_left[:, :, here] = value[half:]

    def store_own(here, value):
        own[:, :, here] = value

    spots = [pl.ds(n * width, width) for n in range(tiles)]
    right, left = h_peer(1), h_peer(nh - 1)
    build(0, (h + 2) % nh)
    for n, here in enumerate(spots):
        if n % 2 == 0:
            multiply(0, store_far, spots[n : n + 2])
        send(send_far.at[lower, :, here], far_left.at[:, :, here], far_send.at[0], far_recv.at[0, n], right)
        send(send_far.at[upper, :, here], far_right.at[:, :, here], far_send.at[1], far_recv.at[1, n], left)
    build(1, (h + 1) % nh)
    build(0, (h + nh - 1) % nh)
    multiply(1, store_right, spots)
    build(1, h)
    multiply(0, store_left, spots)
    multiply(1, store_own, spots)
    send(send_right.at[upper], near_left.at[upper], near_send.at[0], near_recv.at[0], right)
    send(send_left.at[lower], near_right.at[lower], near_send.at[1], near_recv.at[1], left)

    for n, here in enumerate(spots):
        wait(far_left.at[:, :, here], far_recv.at[0, n])
        send_right[:half, :, here] = (hold_right[:, :, here] + far_left[:, :, here].astype(jnp.float32)).astype(
            jnp.bfloat16
        )
        there = (lower, slice(None), here)
        send(send_right.at[there], near_left.at[there], late_send.at[0], late_recv.at[0, n], right)
        wait(far_right.at[:, :, here], far_recv.at[1, n])
        send_left[half:, :, here] = (hold_left[:, :, here] + far_right[:, :, here].astype(jnp.float32)).astype(
            jnp.bfloat16
        )
        there = (upper, slice(None), here)
        send(send_left.at[there], near_right.at[there], late_send.at[1], late_recv.at[1, n], left)

    wait(near_left.at[upper], near_recv.at[0])
    wait(near_right.at[lower], near_recv.at[1])
    for n, here in enumerate(spots):
        wait(near_left.at[lower, :, here], late_recv.at[0, n])
        wait(near_right.at[upper, :, here], late_recv.at[1, n])
        value = own[:, :, here] + near_left[:, :, here].astype(jnp.float32) + near_right[:, :, here].astype(jnp.float32)
        final[:, :, here] = value.astype(jnp.bfloat16)
        for i in range(1, nb):
            send(final.at[b_at(i), :, here], operator.at[b, :, here], op_send, op_recv.at[n], b_peer(i))
    operator[b] = final[b]
    turned = jnp.zeros((block, orbitals), jnp.float32)
    for n, here in enumerate(spots):
        wait(operator.at[pl.ds(0, nb - 1), :, here], op_recv.at[n])
        turned = turned + jnp.dot(
            operator[:, :, here].reshape(block, width), order[here, :], preferred_element_type=jnp.float32
        )
    turned_operator[...] = turned.astype(jnp.bfloat16)

    summed = [first[c * (padded // PARTS) : (c + 1) * (padded // PARTS)] for c in range(PARTS)]
    for degree in range(1, ORDER + 1):
        for c in range(PARTS):
            wait(terms.at[degree - 1, some(c), pl.ds(0, (na - 1) * block)], term_recv.at[degree - 1, c])
            product = lax.dot_general(
                terms[degree - 1, some(c), :],
                turned_operator[...],
                (((1,), (1,)), ((), ())),
                preferred_element_type=jnp.float32,
            )
            term = (product / degree).astype(jnp.bfloat16)
            if degree < ORDER:
                terms[degree, some(c), mine] = term
                share(degree, c)
            summed[c] = summed[c] + term.astype(jnp.float32)

    tall = jnp.concatenate([*summed, jnp.zeros((result.shape[2] - padded, block), jnp.float32)], axis=0)
    result[...] = jnp.transpose(tall).astype(jnp.bfloat16).reshape(result.shape)
    for i in range(1, nb):
        send(result.at[b_at(i)], landed.at[b], out_sem.at[0], out_sem.at[1], b_peer(i))
    landed[b] = result[b]
    wait(landed.at[pl.ds(0, nb - 1)], out_sem.at[1])
    for j in range(nb):
        out_ref[:, j * electrons : (j + 1) * electrons] = landed[j, :, :electrons]

    for i in range(3):
        wait(fb_chunks, fb_send.at[i])
    wait(phi.at[pl.ds(0, nb - 1)], phi_sem.at[0])
    for k in range(ORDER):
        wait(terms.at[k, :, pl.ds(0, (na - 1) * block)], term_send.at[k])
    for sem in (far_send, near_send, late_send):
        wait(far_left, sem.at[0])
        wait(far_right, sem.at[1])
    wait(operator.at[pl.ds(0, nb - 1)], op_send)
    wait(result.at[pl.ds(0, nb - 1)], out_sem.at[0])


def local(na, nb, nh, walkers, inv_intersection, rotated, cholesky, field_noise):
    walker_count, electrons = inv_intersection.shape[:2]
    rows = walkers.shape[0]
    vectors, _, orbitals = cholesky.shape
    wide_electrons = ceil_to(electrons, LANES)
    padded = ceil_to(electrons, 16)
    half = nb // 2
    bf16, f32 = jnp.bfloat16, jnp.float32
    depth = vectors * rows
    dma = pltpu.SemaphoreType.DMA
    vmem = pl.BlockSpec(memory_space=pltpu.VMEM)
    piece = (nb, rows, orbitals)
    fields, propagated = pl.pallas_call(
        functools.partial(kernel, (na, nb, nh, rows, electrons)),
        out_shape=(
            jax.ShapeDtypeStruct((walker_count, vectors), f32),
            jax.ShapeDtypeStruct((rows, nb * electrons), bf16),
        ),
        in_specs=[pl.BlockSpec(memory_space=pltpu.HBM)] * 5,
        out_specs=(vmem, vmem),
        scratch_shapes=[
            pltpu.VMEM(walkers.shape, bf16),
            pltpu.VMEM((electrons, walker_count, electrons), bf16),
            pltpu.VMEM((electrons * rows, vectors), bf16),
            pltpu.VMEM((depth, orbitals), bf16),
            pltpu.VMEM((walker_count, vectors), f32),
            pltpu.VMEM((ceil_to(electrons, 8) * walker_count, LANES), f32),
            pltpu.VMEM((ceil_to(electrons, 8) * walker_count, LANES), f32),
            pltpu.VMEM((walker_count, rows, electrons), bf16),
            pltpu.VMEM((walker_count * rows, electrons * rows), bf16),
            pltpu.VMEM((walker_count, vectors), f32),
            pltpu.VMEM((nb, rows, wide_electrons), bf16),
            pltpu.VMEM((vectors, depth), bf16),
            pltpu.VMEM((orbitals, orbitals), bf16),
            pltpu.VMEM((walker_count, depth), f32),
            pltpu.VMEM((2, nb * rows, depth), bf16),
            pltpu.VMEM((na, 8, LANES), f32),
            pltpu.VMEM((nb, 8, LANES), f32),
            pltpu.VMEM((walker_count, vectors), f32),
            pltpu.VMEM((nb, rows, wide_electrons), bf16),
            pltpu.VMEM((ORDER, padded, orbitals), bf16),
            pltpu.VMEM(piece, bf16),
            pltpu.VMEM(piece, bf16),
            pltpu.VMEM(piece, bf16),
            pltpu.VMEM((half, rows, orbitals), f32),
            pltpu.VMEM((half, rows, orbitals), f32),
            pltpu.VMEM(piece, f32),
            pltpu.VMEM((half, rows, orbitals), bf16),
            pltpu.VMEM((half, rows, orbitals), bf16),
            pltpu.VMEM(piece, bf16),
            pltpu.VMEM(piece, bf16),
            pltpu.VMEM(piece, bf16),
            pltpu.VMEM(piece, bf16),
            pltpu.VMEM((nb * rows, orbitals), bf16),
            pltpu.VMEM((nb, rows, wide_electrons), bf16),
            pltpu.VMEM((nb, rows, wide_electrons), bf16),
            dma((5,)),
            dma((3,)),
            dma((3,)),
            dma((2,)),
            dma((ORDER,)),
            dma((ORDER, PARTS)),
            dma((2,)),
            dma((2, 4)),
            dma((2,)),
            dma((2,)),
            dma((2,)),
            dma((2, 4)),
            dma,
            dma((4,)),
            dma((2,)),
        ],
        compiler_params=pltpu.CompilerParams(
            collective_id=0, has_side_effects=True, vmem_limit_bytes=48 * 1024 * 1024
        ),
    )(
        *(
            pltpu.with_memory_space_constraint(array, pltpu.HBM)
            for array in (
                walkers,
                jnp.transpose(inv_intersection, (1, 0, 2)),
                jnp.transpose(rotated, (2, 1, 0)).reshape(electrons * rows, vectors),
                cholesky.reshape(depth, orbitals),
                field_noise,
            )
        )
    )
    return fields, propagated


def solution(mesh):
    nh = mesh.shape["vec"]
    nb = 8 if mesh.shape["rows"] == 64 else 2
    na = mesh.shape["rows"] // nb
    placed = (P("rows", None), P(), P("vec", "rows", None), P("vec", "rows", None), P(None, "vec"))
    return jax.shard_map(
        functools.partial(local, na, nb, nh),
        mesh=mesh,
        in_specs=placed,
        out_specs=(P(None, "vec"), P("rows", "vec")),
        check_vma=False,
    )
```

```python
import functools

import jax
import jax.numpy as jnp
from jax import lax
from jax.experimental import pallas as pl
from jax.experimental.pallas import tpu as pltpu
from jax.sharding import PartitionSpec as P

MESH = pl.DeviceIdType.MESH
ORDER = 4
LANES = 128
TILE = 256
PARTS = 5

time_root = 0.1


def ceil_to(value, unit):
    return -(-value // unit) * unit


def place(nb, r):
    if nb == 2:
        return r % 2, r // 2
    x, y, low = r // 16, (r // 4) % 4, r % 4
    return ((y + y // 2) % 2) * 4 + low, x * 2 + y // 2


def device(nb, a, b):
    if nb == 2:
        return b * 2 + a
    x, half = b // 2, b % 2
    return x * 16 + (2 * half + (a // 4 + half) % 2) * 4 + a % 4


def kernel(
    dims,
    walkers_hbm,
    inverse_hbm,
    rotated_hbm,
    chol_hbm,
    noise_hbm,
    fields_ref,
    out_ref,
    walkers,
    inverse,
    rotated,
    chol,
    noise,
    wide_low,
    wide_high,
    mixed,
    mixed_diag,
    part,
    phi,
    spread,
    order,
    wide,
    diag,
    fb_one,
    fb_two,
    fb_all,
    phi_block,
    terms,
    send_far,
    send_right,
    send_left,
    hold_right,
    hold_left,
    own,
    far_left,
    far_right,
    op_own,
    op_early,
    op_late,
    turned_operator,
    result,
    landed,
    load_sem,
    fb_send,
    fb_recv,
    phi_sem,
    term_send,
    term_recv,
    far_send,
    far_recv,
    early_send,
    early_recv,
    own_send,
    own_recv,
    late_send,
    late_recv,
    out_sem,
):
    na, nb, nh, rows, electrons = dims
    half = nb // 2
    block = nb * rows
    depth = chol.shape[0]
    orbitals = chol.shape[1]
    padded = terms.shape[1]
    r = lax.axis_index("rows")
    h = lax.axis_index("vec")
    a, b = place(nb, r)

    def a_at(i):
        return sum(((a // bit) % 2 if not (na - i) // bit % 2 else 1 - (a // bit) % 2) * bit for bit in (4, 2, 1) if bit < na)

    def b_at(i):
        if nb == 2:
            return 1 - b
        step, turn = ((2, 1), (1, 1), (3, 1), (2, 0), (1, 0), (3, 0), (0, 1))[i - 1]
        return (b // 2 + step) % 4 * 2 + (1 - b % 2 if turn else b % 2)

    def a_peer(i):
        return (device(nb, a_at(i), b), h)

    def b_peer(i):
        return (device(nb, a, b_at(i)), h)

    def h_peer(i):
        return (r, (h + i) % nh)

    def send(src, dst, send_sem, recv_sem, peer):
        copy = pltpu.make_async_remote_copy(
            src_ref=src, dst_ref=dst, send_sem=send_sem, recv_sem=recv_sem, device_id=peer, device_id_type=MESH
        )
        copy.start()

    def wait(span, sem):
        pltpu.make_async_copy(span, span, sem).wait()

    def chunk(c):
        return (pl.ds(pl.multiple_of((c // 2) * 8, 8), 8), pl.ds(pl.multiple_of((c % 2) * LANES, LANES), LANES))

    pairs = ((walkers_hbm, walkers), (inverse_hbm, inverse), (rotated_hbm, rotated), (chol_hbm, chol), (noise_hbm, noise))
    loads = [pltpu.make_async_copy(src, dst, load_sem.at[i]) for i, (src, dst) in enumerate(pairs)]
    for load in loads:
        load.start()

    barrier = pltpu.get_barrier_semaphore()
    def owner(j, step):
        return (device(nb, a, j), (h + step) % nh)

    peers = [a_peer(i) for i in range(1, na)] + [b_peer(i) for i in range(1, nb)]
    peers += [owner(j, step) for j in range(nb) for step in (1, nh - 1)]
    for peer in peers:
        pl.semaphore_signal(barrier, inc=1, device_id=peer, device_id_type=MESH)
    def fill(k, _):
        row = lax.broadcasted_iota(jnp.int32, (spread.shape[0], TILE), 0)
        lane = lax.broadcasted_iota(jnp.int32, (spread.shape[0], TILE), 1)
        here = row == (TILE // rows) * k + lane // rows
        spread[:, pl.ds(pl.multiple_of(k * TILE, TILE), TILE)] = jnp.where(here, 1.0, 0.0).astype(jnp.bfloat16)
        return 0

    lax.fori_loop(0, depth // TILE, fill, 0)

    count = mixed.shape[0]
    span = electrons * rows
    loads[1].wait()
    wide_low[: electrons * count, :] = inverse[:, :, :LANES].astype(jnp.float32).reshape(electrons * count, LANES)
    wide_high[: electrons * count, : electrons - LANES] = (
        inverse[:, :, LANES:].astype(jnp.float32).reshape(electrons * count, electrons - LANES)
    )
    loads[0].wait()
    for w in range(count):
        low = wide_low[pl.ds(w, ceil_to(electrons, 8), stride=count), :]
        high = wide_high[pl.ds(w, ceil_to(electrons, 8), stride=count), :]
        matrix = jnp.concatenate([low, high], axis=1).astype(jnp.bfloat16)[:electrons, :electrons]
        mixed[w] = jnp.dot(
            walkers[:, w * electrons : (w + 1) * electrons], matrix, preferred_element_type=jnp.float32
        ).astype(jnp.bfloat16)
    for start in range(0, span, TILE):
        here = pl.ds(start, min(TILE, span - start))
        spaced = jnp.dot(
            mixed[...].reshape(count * rows, electrons), spread[:electrons, here], preferred_element_type=jnp.float32
        )
        p = lax.broadcasted_iota(jnp.int32, spaced.shape, 0) % rows
        lane = lax.broadcasted_iota(jnp.int32, spaced.shape, 1) % rows
        mixed_diag[:, here] = jnp.where(p == lane, spaced, 0.0).astype(jnp.bfloat16)
    phi[:, :, LANES:] = jnp.zeros((nb, rows, phi.shape[2] - LANES), jnp.bfloat16)
    for k in range(nh):

        @pl.when(h == k)
        def _():
            for j in range(nb):
                start = (k * nb + j) * electrons
                phi[j, :, :electrons] = walkers[:, start : start + electrons]

    pl.semaphore_wait(barrier, len(peers))

    for i in range(1, nb):
        send(phi.at[b_at(i)], phi_block.at[b], phi_sem.at[0], phi_sem.at[1], b_peer(i))
    phi_block[b] = phi[b]
    loads[2].wait()
    by_row = jnp.dot(mixed_diag[...], rotated[...], preferred_element_type=jnp.float32)
    part[...] = jnp.sum(by_row.reshape(count, rows, by_row.shape[1]), axis=1)

    for i in range(1, na):
        send(part.at[chunk(a_at(i))], fb_one.at[i], fb_send.at[0], fb_recv.at[0], a_peer(i))

    def arrange(k, _):
        lane = lax.broadcasted_iota(jnp.int32, (1, block), 1)
        source = device(nb, k, lane // rows) * rows + lane % rows
        row = lax.broadcasted_iota(jnp.int32, (orbitals, block), 0)
        here = pl.ds(pl.multiple_of(k * block, block), block)
        order[:, here] = jnp.where(row == source, 1.0, 0.0).astype(jnp.bfloat16)
        return 0

    lax.fori_loop(0, na, arrange, 0)

    fb_chunks = fb_one.at[pl.ds(1, na - 1)]
    wait(fb_chunks, fb_recv.at[0])
    total = part[chunk(a)]
    for i in range(1, na):
        total = total + fb_one[i]
    fb_two[b] = total
    for i in range(1, nb):
        send(fb_two.at[b], fb_two.at[b], fb_send.at[1], fb_recv.at[1], b_peer(i))

    wait(phi_block.at[pl.ds(0, nb - 1)], phi_sem.at[1])
    mine = pl.ds(pl.multiple_of(a * block, block), block)
    turned = jnp.transpose(phi_block[...].reshape(block, phi_block.shape[2]).astype(jnp.float32))
    first = turned[:padded, :]
    terms[0, :, mine] = first.astype(jnp.bfloat16)

    def some(c):
        return pl.ds(c * (padded // PARTS), padded // PARTS)

    def share(k, c):
        there = terms.at[k, some(c), mine]
        for i in range(1, na):
            send(there, there, term_send.at[k], term_recv.at[k, c], a_peer(i))

    for c in range(PARTS):
        share(0, c)

    wait(fb_two.at[pl.ds(0, nb - 1)], fb_recv.at[1])
    total = fb_two[0]
    for i in range(1, nb):
        total = total + fb_two[i]
    fb_all[chunk(a)] = total
    for i in range(1, na):
        send(fb_all.at[chunk(a)], fb_all.at[chunk(a)], fb_send.at[2], fb_recv.at[2], a_peer(i))

    wait(fb_chunks, fb_recv.at[2])
    loads[4].wait()
    fields = noise[...] - time_root * fb_all[...]
    fields_ref[...] = fields
    scaled = (-time_root * fields).astype(jnp.bfloat16)

    wide[...] = jnp.dot(scaled, spread[...], preferred_element_type=jnp.float32)
    loads[3].wait()

    lower, upper = pl.ds(0, half), pl.ds(half, half)
    width = min(TILE, orbitals)
    tiles = orbitals // width

    def build(slot, c):
        p = lax.broadcasted_iota(jnp.int32, (rows, depth), 0)
        lane = lax.broadcasted_iota(jnp.int32, (rows, depth), 1)
        for w in range(nb):
            row = jnp.broadcast_to(wide[pl.ds(c * nb + w, 1), :], (rows, depth))
            diag[slot, w * rows : (w + 1) * rows, :] = jnp.where(p == lane % rows, row, 0.0).astype(jnp.bfloat16)

    def multiply(slot, store, some_spots):
        for here in some_spots:
            product = jnp.dot(diag[slot], chol[:, here], preferred_element_type=jnp.float32)
            store(here, product.reshape(nb, rows, width))

    def store_far(here, value):
        send_far[:, :, here] = value.astype(jnp.bfloat16)

    def store_right(here, value):
        hold_right[:, :, here] = value[:half]
        send_right[half:, :, here] = value[half:].astype(jnp.bfloat16)

    def store_left(here, value):
        send_left[:half, :, here] = value[:half].astype(jnp.bfloat16)
        hold_left[:, :, here] = value[half:]

    def store_own(here, value):
        own[:, :, here] = value.astype(jnp.bfloat16)

    spots = [pl.ds(n * width, width) for n in range(tiles)]
    right, left = h_peer(1), h_peer(nh - 1)
    build(0, (h + 2) % nh)
    for n, here in enumerate(spots):
        if n < 2:
            multiply(0, store_far, spots[:1] if n == 0 else spots[1:])
        send(send_far.at[lower, :, here], far_left.at[:, :, here], far_send.at[0], far_recv.at[0, n], right)
        send(send_far.at[upper, :, here], far_right.at[:, :, here], far_send.at[1], far_recv.at[1, n], left)
    build(1, (h + 1) % nh)
    build(0, (h + nh - 1) % nh)
    multiply(1, store_right, spots)
    build(1, h)
    multiply(0, store_left, spots)
    multiply(1, store_own, spots)
    for j in range(half):
        k = half + j
        send(send_right.at[k], op_early.at[b], early_send, early_recv, owner(k, 1))
        send(send_left.at[j], op_early.at[b], early_send, early_recv, owner(j, nh - 1))
    for i in range(1, nb):
        send(own.at[b_at(i)], op_own.at[b], own_send, own_recv, b_peer(i))
    op_own[b] = own[b]

    for n, here in enumerate(spots):
        wait(far_left.at[:, :, here], far_recv.at[0, n])
        send_right[:half, :, here] = (hold_right[:, :, here] + far_left[:, :, here].astype(jnp.float32)).astype(
            jnp.bfloat16
        )
        for j in range(half):
            send(send_right.at[j, :, here], op_late.at[b, :, here], late_send, late_recv.at[n], owner(j, 1))
        wait(far_right.at[:, :, here], far_recv.at[1, n])
        send_left[half:, :, here] = (hold_left[:, :, here] + far_right[:, :, here].astype(jnp.float32)).astype(
            jnp.bfloat16
        )
        for k in range(half, nb):
            send(send_left.at[k, :, here], op_late.at[b, :, here], late_send, late_recv.at[n], owner(k, nh - 1))

    wait(op_own.at[pl.ds(0, nb - 1)], own_recv)
    wait(op_early, early_recv)
    turned = jnp.zeros((block, orbitals), jnp.float32)
    for n, here in enumerate(spots):
        wait(op_late.at[:, :, here], late_recv.at[n])
        value = op_own[:, :, here].astype(jnp.float32) + op_early[:, :, here].astype(jnp.float32)
        value = (value + op_late[:, :, here].astype(jnp.float32)).astype(jnp.bfloat16)
        turned = turned + jnp.dot(value.reshape(block, width), order[here, :], preferred_element_type=jnp.float32)
    turned_operator[...] = turned.astype(jnp.bfloat16)

    summed = [first[c * (padded // PARTS) : (c + 1) * (padded // PARTS)] for c in range(PARTS)]
    for degree in range(1, ORDER + 1):
        for c in range(PARTS):
            wait(terms.at[degree - 1, some(c), pl.ds(0, (na - 1) * block)], term_recv.at[degree - 1, c])
            product = lax.dot_general(
                terms[degree - 1, some(c), :],
                turned_operator[...],
                (((1,), (1,)), ((), ())),
                preferred_element_type=jnp.float32,
            )
            term = (product / degree).astype(jnp.bfloat16)
            if degree < ORDER:
                terms[degree, some(c), mine] = term
                share(degree, c)
            summed[c] = summed[c] + term.astype(jnp.float32)

    tall = jnp.concatenate([*summed, jnp.zeros((result.shape[2] - padded, block), jnp.float32)], axis=0)
    result[...] = jnp.transpose(tall).astype(jnp.bfloat16).reshape(result.shape)
    for i in range(1, nb):
        send(result.at[b_at(i)], landed.at[b], out_sem.at[0], out_sem.at[1], b_peer(i))
    landed[b] = result[b]
    wait(landed.at[pl.ds(0, nb - 1)], out_sem.at[1])
    for j in range(nb):
        out_ref[:, j * electrons : (j + 1) * electrons] = landed[j, :, :electrons]

    for i in range(3):
        wait(fb_chunks, fb_send.at[i])
    wait(phi.at[pl.ds(0, nb - 1)], phi_sem.at[0])
    for k in range(ORDER):
        wait(terms.at[k, :, pl.ds(0, (na - 1) * block)], term_send.at[k])
    wait(far_left, far_send.at[0])
    wait(far_right, far_send.at[1])
    wait(op_early, early_send)
    wait(op_late, late_send)
    wait(op_own.at[pl.ds(0, nb - 1)], own_send)
    wait(result.at[pl.ds(0, nb - 1)], out_sem.at[0])


def local(na, nb, nh, walkers, inv_intersection, rotated, cholesky, field_noise):
    walker_count, electrons = inv_intersection.shape[:2]
    rows = walkers.shape[0]
    vectors, _, orbitals = cholesky.shape
    wide_electrons = ceil_to(electrons, LANES)
    padded = ceil_to(electrons, 16)
    half = nb // 2
    bf16, f32 = jnp.bfloat16, jnp.float32
    depth = vectors * rows
    dma = pltpu.SemaphoreType.DMA
    vmem = pl.BlockSpec(memory_space=pltpu.VMEM)
    piece = (nb, rows, orbitals)
    fields, propagated = pl.pallas_call(
        functools.partial(kernel, (na, nb, nh, rows, electrons)),
        out_shape=(
            jax.ShapeDtypeStruct((walker_count, vectors), f32),
            jax.ShapeDtypeStruct((rows, nb * electrons), bf16),
        ),
        in_specs=[pl.BlockSpec(memory_space=pltpu.HBM)] * 5,
        out_specs=(vmem, vmem),
        scratch_shapes=[
            pltpu.VMEM(walkers.shape, bf16),
            pltpu.VMEM((electrons, walker_count, electrons), bf16),
            pltpu.VMEM((electrons * rows, vectors), bf16),
            pltpu.VMEM((depth, orbitals), bf16),
            pltpu.VMEM((walker_count, vectors), f32),
            pltpu.VMEM((ceil_to(electrons, 8) * walker_count, LANES), f32),
            pltpu.VMEM((ceil_to(electrons, 8) * walker_count, LANES), f32),
            pltpu.VMEM((walker_count, rows, electrons), bf16),
            pltpu.VMEM((walker_count * rows, electrons * rows), bf16),
            pltpu.VMEM((walker_count, vectors), f32),
            pltpu.VMEM((nb, rows, wide_electrons), bf16),
            pltpu.VMEM((vectors, depth), bf16),
            pltpu.VMEM((orbitals, orbitals), bf16),
            pltpu.VMEM((walker_count, depth), f32),
            pltpu.VMEM((2, nb * rows, depth), bf16),
            pltpu.VMEM((na, 8, LANES), f32),
            pltpu.VMEM((nb, 8, LANES), f32),
            pltpu.VMEM((walker_count, vectors), f32),
            pltpu.VMEM((nb, rows, wide_electrons), bf16),
            pltpu.VMEM((ORDER, padded, orbitals), bf16),
            pltpu.VMEM(piece, bf16),
            pltpu.VMEM(piece, bf16),
            pltpu.VMEM(piece, bf16),
            pltpu.VMEM((half, rows, orbitals), f32),
            pltpu.VMEM((half, rows, orbitals), f32),
            pltpu.VMEM(piece, bf16),
            pltpu.VMEM((half, rows, orbitals), bf16),
            pltpu.VMEM((half, rows, orbitals), bf16),
            pltpu.VMEM(piece, bf16),
            pltpu.VMEM(piece, bf16),
            pltpu.VMEM(piece, bf16),
            pltpu.VMEM((nb * rows, orbitals), bf16),
            pltpu.VMEM((nb, rows, wide_electrons), bf16),
            pltpu.VMEM((nb, rows, wide_electrons), bf16),
            dma((5,)),
            dma((3,)),
            dma((3,)),
            dma((2,)),
            dma((ORDER,)),
            dma((ORDER, PARTS)),
            dma((2,)),
            dma((2, 4)),
            dma,
            dma,
            dma,
            dma,
            dma,
            dma((4,)),
            dma((2,)),
        ],
        compiler_params=pltpu.CompilerParams(
            collective_id=0, has_side_effects=True, vmem_limit_bytes=48 * 1024 * 1024
        ),
    )(
        *(
            pltpu.with_memory_space_constraint(array, pltpu.HBM)
            for array in (
                walkers,
                jnp.transpose(inv_intersection, (1, 0, 2)),
                jnp.transpose(rotated, (2, 1, 0)).reshape(electrons * rows, vectors),
                cholesky.reshape(depth, orbitals),
                field_noise,
            )
        )
    )
    return fields, propagated


def solution(mesh):
    nh = mesh.shape["vec"]
    nb = 8 if mesh.shape["rows"] == 64 else 2
    na = mesh.shape["rows"] // nb
    placed = (P("rows", None), P(), P("vec", "rows", None), P("vec", "rows", None), P(None, "vec"))
    return jax.shard_map(
        functools.partial(local, na, nb, nh),
        mesh=mesh,
        in_specs=placed,
        out_specs=(P(None, "vec"), P("rows", "vec")),
        check_vma=False,
    )
```

```python
import functools

import jax
import jax.numpy as jnp
from jax import lax
from jax.experimental import pallas as pl
from jax.experimental.pallas import tpu as pltpu
from jax.sharding import PartitionSpec as P

MESH = pl.DeviceIdType.MESH
ORDER = 4
LANES = 128
TILE = 256
PARTS = 5

time_root = 0.1


def ceil_to(value, unit):
    return -(-value // unit) * unit


def place(nb, r):
    if nb == 2:
        return r % 2, r // 2
    x, y, low = r // 16, (r // 4) % 4, r % 4
    return ((y + y // 2) % 2) * 4 + low, x * 2 + y // 2


def device(nb, a, b):
    if nb == 2:
        return b * 2 + a
    x, half = b // 2, b % 2
    return x * 16 + (2 * half + (a // 4 + half) % 2) * 4 + a % 4


def kernel(
    dims,
    walkers_hbm,
    inverse_hbm,
    rotated_hbm,
    chol_hbm,
    noise_hbm,
    fields_ref,
    out_ref,
    walkers,
    inverse,
    rotated,
    chol,
    noise,
    by_walker,
    mixed,
    mixed_diag,
    part,
    phi,
    spread,
    order,
    wide,
    diag,
    fb_one,
    fb_two,
    fb_all,
    phi_block,
    terms,
    send_far,
    send_right,
    send_left,
    hold_right,
    hold_left,
    own,
    far_left,
    far_right,
    op_own,
    op_early,
    op_late,
    turned_operator,
    result,
    landed,
    load_sem,
    fb_send,
    fb_recv,
    phi_sem,
    term_send,
    term_recv,
    far_send,
    far_recv,
    early_send,
    early_recv,
    own_send,
    own_recv,
    late_send,
    late_recv,
    out_sem,
):
    na, nb, nh, rows, electrons = dims
    half = nb // 2
    block = nb * rows
    depth = chol.shape[0]
    orbitals = chol.shape[1]
    padded = terms.shape[1]
    r = lax.axis_index("rows")
    h = lax.axis_index("vec")
    a, b = place(nb, r)

    def a_at(i):
        return sum(((a // bit) % 2 if not (na - i) // bit % 2 else 1 - (a // bit) % 2) * bit for bit in (4, 2, 1) if bit < na)

    def b_at(i):
        if nb == 2:
            return 1 - b
        step, turn = ((2, 1), (1, 1), (3, 1), (2, 0), (1, 0), (3, 0), (0, 1))[i - 1]
        return (b // 2 + step) % 4 * 2 + (1 - b % 2 if turn else b % 2)

    def a_peer(i):
        return (device(nb, a_at(i), b), h)

    def b_peer(i):
        return (device(nb, a, b_at(i)), h)

    def h_peer(i):
        return (r, (h + i) % nh)

    def send(src, dst, send_sem, recv_sem, peer):
        copy = pltpu.make_async_remote_copy(
            src_ref=src, dst_ref=dst, send_sem=send_sem, recv_sem=recv_sem, device_id=peer, device_id_type=MESH
        )
        copy.start()

    def wait(span, sem):
        pltpu.make_async_copy(span, span, sem).wait()

    def chunk(c):
        return (pl.ds(pl.multiple_of((c // 2) * 8, 8), 8), pl.ds(pl.multiple_of((c % 2) * LANES, LANES), LANES))

    pairs = ((walkers_hbm, walkers), (inverse_hbm, inverse), (rotated_hbm, rotated), (chol_hbm, chol), (noise_hbm, noise))
    loads = [pltpu.make_async_copy(src, dst, load_sem.at[i]) for i, (src, dst) in enumerate(pairs)]
    for i in (1, 0, 2):
        loads[i].start()

    barrier = pltpu.get_barrier_semaphore()
    def owner(j, step):
        return (device(nb, a, j), (h + step) % nh)

    peers = [a_peer(i) for i in range(1, na)] + [b_peer(i) for i in range(1, nb)]
    peers += [owner(j, step) for j in range(nb) for step in (1, nh - 1)]
    for peer in peers:
        pl.semaphore_signal(barrier, inc=1, device_id=peer, device_id_type=MESH)
    def fill(k, _):
        row = lax.broadcasted_iota(jnp.int32, (spread.shape[0], TILE), 0)
        lane = lax.broadcasted_iota(jnp.int32, (spread.shape[0], TILE), 1)
        here = row == (TILE // rows) * k + lane // rows
        spread[:, pl.ds(pl.multiple_of(k * TILE, TILE), TILE)] = jnp.where(here, 1.0, 0.0).astype(jnp.bfloat16)
        return 0

    lax.fori_loop(0, depth // TILE, fill, 0)

    count = mixed.shape[0]
    span = electrons * rows
    to = lax.broadcasted_iota(jnp.int32, (8 * count, 8 * count), 0)
    source = lax.broadcasted_iota(jnp.int32, (8 * count, 8 * count), 1)
    gather = jnp.where(source == (to % 8) * count + to // 8, 1.0, 0.0).astype(jnp.bfloat16)
    loads[1].wait()

    def eight(f):
        size = min(8, electrons - f)
        if size <= 0:
            return jnp.zeros((count, 8, electrons), jnp.float32)
        taken = inverse[f : f + size].reshape(size * count, electrons)
        return jnp.dot(gather[:, : size * count], taken, preferred_element_type=jnp.float32).reshape(count, 8, electrons)

    for f in range(0, electrons, 16):
        by_walker[:, f : f + 16, :] = jnp.concatenate([eight(f), eight(f + 8)], axis=1).astype(jnp.bfloat16)
    loads[0].wait()
    for w in range(count):
        mixed[w] = jnp.dot(
            walkers[:, w * electrons : (w + 1) * electrons],
            by_walker[w, :electrons, :],
            preferred_element_type=jnp.float32,
        ).astype(jnp.bfloat16)
    for start in range(0, span, TILE):
        here = pl.ds(start, min(TILE, span - start))
        spaced = jnp.dot(
            mixed[...].reshape(count * rows, electrons), spread[:electrons, here], preferred_element_type=jnp.float32
        )
        p = lax.broadcasted_iota(jnp.int32, spaced.shape, 0) % rows
        lane = lax.broadcasted_iota(jnp.int32, spaced.shape, 1) % rows
        mixed_diag[:, here] = jnp.where(p == lane, spaced, 0.0).astype(jnp.bfloat16)
    loads[3].start()
    loads[4].start()
    loads[2].wait()
    by_row = jnp.dot(mixed_diag[...], rotated[...], preferred_element_type=jnp.float32)
    part[...] = jnp.sum(by_row.reshape(count, rows, by_row.shape[1]), axis=1)

    pl.semaphore_wait(barrier, len(peers))

    for i in range(1, na):
        send(part.at[chunk(a_at(i))], fb_one.at[i], fb_send.at[0], fb_recv.at[0], a_peer(i))

    phi[:, :, LANES:] = jnp.zeros((nb, rows, phi.shape[2] - LANES), jnp.bfloat16)
    for k in range(nh):

        @pl.when(h == k)
        def _():
            for j in range(nb):
                start = (k * nb + j) * electrons
                phi[j, :, :electrons] = walkers[:, start : start + electrons]

    for i in range(1, nb):
        send(phi.at[b_at(i)], phi_block.at[b], phi_sem.at[0], phi_sem.at[1], b_peer(i))
    phi_block[b] = phi[b]

    def arrange(k, _):
        lane = lax.broadcasted_iota(jnp.int32, (1, block), 1)
        source = device(nb, k, lane // rows) * rows + lane % rows
        row = lax.broadcasted_iota(jnp.int32, (orbitals, block), 0)
        here = pl.ds(pl.multiple_of(k * block, block), block)
        order[:, here] = jnp.where(row == source, 1.0, 0.0).astype(jnp.bfloat16)
        return 0

    lax.fori_loop(0, na, arrange, 0)

    fb_chunks = fb_one.at[pl.ds(1, na - 1)]
    wait(fb_chunks, fb_recv.at[0])
    total = part[chunk(a)]
    for i in range(1, na):
        total = total + fb_one[i]
    fb_two[b] = total
    for i in range(1, nb):
        send(fb_two.at[b], fb_two.at[b], fb_send.at[1], fb_recv.at[1], b_peer(i))

    wait(phi_block.at[pl.ds(0, nb - 1)], phi_sem.at[1])
    mine = pl.ds(pl.multiple_of(a * block, block), block)
    turned = jnp.transpose(phi_block[...].reshape(block, phi_block.shape[2]).astype(jnp.float32))
    first = turned[:padded, :]
    terms[0, :, mine] = first.astype(jnp.bfloat16)

    def some(c):
        return pl.ds(c * (padded // PARTS), padded // PARTS)

    def share(k, c):
        there = terms.at[k, some(c), mine]
        for i in range(1, na):
            send(there, there, term_send.at[k], term_recv.at[k, c], a_peer(i))

    for c in range(PARTS):
        share(0, c)

    wait(fb_two.at[pl.ds(0, nb - 1)], fb_recv.at[1])
    total = fb_two[0]
    for i in range(1, nb):
        total = total + fb_two[i]
    fb_all[chunk(a)] = total
    for i in range(1, na):
        send(fb_all.at[chunk(a)], fb_all.at[chunk(a)], fb_send.at[2], fb_recv.at[2], a_peer(i))

    wait(fb_chunks, fb_recv.at[2])
    loads[4].wait()
    fields = noise[...] - time_root * fb_all[...]
    fields_ref[...] = fields
    scaled = (-time_root * fields).astype(jnp.bfloat16)

    wide[...] = jnp.dot(scaled, spread[...], preferred_element_type=jnp.float32)
    loads[3].wait()

    lower, upper = pl.ds(0, half), pl.ds(half, half)
    width = min(TILE, orbitals)
    tiles = orbitals // width

    def build(slot, c):
        p = lax.broadcasted_iota(jnp.int32, (rows, depth), 0)
        lane = lax.broadcasted_iota(jnp.int32, (rows, depth), 1)
        for w in range(nb):
            row = jnp.broadcast_to(wide[pl.ds(c * nb + w, 1), :], (rows, depth))
            diag[slot, w * rows : (w + 1) * rows, :] = jnp.where(p == lane % rows, row, 0.0).astype(jnp.bfloat16)

    def multiply(slot, store, some_spots):
        for here in some_spots:
            product = jnp.dot(diag[slot], chol[:, here], preferred_element_type=jnp.float32)
            store(here, product.reshape(nb, rows, width))

    def store_far(here, value):
        send_far[:, :, here] = value.astype(jnp.bfloat16)

    def store_right(here, value):
        hold_right[:, :, here] = value[:half]
        send_right[half:, :, here] = value[half:].astype(jnp.bfloat16)

    def store_left(here, value):
        send_left[:half, :, here] = value[:half].astype(jnp.bfloat16)
        hold_left[:, :, here] = value[half:]

    def store_own(here, value):
        own[:, :, here] = value.astype(jnp.bfloat16)

    spots = [pl.ds(n * width, width) for n in range(tiles)]
    right, left = h_peer(1), h_peer(nh - 1)
    build(0, (h + 2) % nh)
    for n, here in enumerate(spots):
        if n < 2:
            multiply(0, store_far, spots[:1] if n == 0 else spots[1:])
        send(send_far.at[lower, :, here], far_left.at[:, :, here], far_send.at[0], far_recv.at[0, n], right)
        send(send_far.at[upper, :, here], far_right.at[:, :, here], far_send.at[1], far_recv.at[1, n], left)
    build(1, (h + 1) % nh)
    build(0, (h + nh - 1) % nh)
    multiply(1, store_right, spots)
    build(1, h)
    multiply(0, store_left, spots)
    multiply(1, store_own, spots)
    for j in range(half):
        k = half + j
        send(send_right.at[k], op_early.at[b], early_send, early_recv, owner(k, 1))
        send(send_left.at[j], op_early.at[b], early_send, early_recv, owner(j, nh - 1))
    for i in range(1, nb):
        send(own.at[b_at(i)], op_own.at[b], own_send, own_recv, b_peer(i))
    op_own[b] = own[b]

    for n, here in enumerate(spots):
        wait(far_left.at[:, :, here], far_recv.at[0, n])
        send_right[:half, :, here] = (hold_right[:, :, here] + far_left[:, :, here].astype(jnp.float32)).astype(
            jnp.bfloat16
        )
        for j in range(half):
            send(send_right.at[j, :, here], op_late.at[b, :, here], late_send, late_recv.at[n], owner(j, 1))
        wait(far_right.at[:, :, here], far_recv.at[1, n])
        send_left[half:, :, here] = (hold_left[:, :, here] + far_right[:, :, here].astype(jnp.float32)).astype(
            jnp.bfloat16
        )
        for k in range(half, nb):
            send(send_left.at[k, :, here], op_late.at[b, :, here], late_send, late_recv.at[n], owner(k, nh - 1))

    wait(op_own.at[pl.ds(0, nb - 1)], own_recv)
    wait(op_early, early_recv)
    turned = jnp.zeros((block, orbitals), jnp.float32)
    for n, here in enumerate(spots):
        wait(op_late.at[:, :, here], late_recv.at[n])
        value = op_own[:, :, here].astype(jnp.float32) + op_early[:, :, here].astype(jnp.float32)
        value = (value + op_late[:, :, here].astype(jnp.float32)).astype(jnp.bfloat16)
        turned = turned + jnp.dot(value.reshape(block, width), order[here, :], preferred_element_type=jnp.float32)
    turned_operator[...] = turned.astype(jnp.bfloat16)

    summed = [first[c * (padded // PARTS) : (c + 1) * (padded // PARTS)] for c in range(PARTS)]
    for degree in range(1, ORDER + 1):
        for c in range(PARTS):
            wait(terms.at[degree - 1, some(c), pl.ds(0, (na - 1) * block)], term_recv.at[degree - 1, c])
            product = lax.dot_general(
                terms[degree - 1, some(c), :],
                turned_operator[...],
                (((1,), (1,)), ((), ())),
                preferred_element_type=jnp.float32,
            )
            term = (product / degree).astype(jnp.bfloat16)
            if degree < ORDER:
                terms[degree, some(c), mine] = term
                share(degree, c)
            summed[c] = summed[c] + term.astype(jnp.float32)

    tall = jnp.concatenate([*summed, jnp.zeros((result.shape[2] - padded, block), jnp.float32)], axis=0)
    result[...] = jnp.transpose(tall).astype(jnp.bfloat16).reshape(result.shape)
    for i in range(1, nb):
        send(result.at[b_at(i)], landed.at[b], out_sem.at[0], out_sem.at[1], b_peer(i))
    landed[b] = result[b]
    wait(landed.at[pl.ds(0, nb - 1)], out_sem.at[1])
    for j in range(nb):
        out_ref[:, j * electrons : (j + 1) * electrons] = landed[j, :, :electrons]

    for i in range(3):
        wait(fb_chunks, fb_send.at[i])
    wait(phi.at[pl.ds(0, nb - 1)], phi_sem.at[0])
    for k in range(ORDER):
        wait(terms.at[k, :, pl.ds(0, (na - 1) * block)], term_send.at[k])
    wait(far_left, far_send.at[0])
    wait(far_right, far_send.at[1])
    wait(op_early, early_send)
    wait(op_late, late_send)
    wait(op_own.at[pl.ds(0, nb - 1)], own_send)
    wait(result.at[pl.ds(0, nb - 1)], out_sem.at[0])


def local(na, nb, nh, walkers, inv_intersection, rotated, cholesky, field_noise):
    walker_count, electrons = inv_intersection.shape[:2]
    rows = walkers.shape[0]
    vectors, _, orbitals = cholesky.shape
    wide_electrons = ceil_to(electrons, LANES)
    padded = ceil_to(electrons, 16)
    half = nb // 2
    bf16, f32 = jnp.bfloat16, jnp.float32
    depth = vectors * rows
    dma = pltpu.SemaphoreType.DMA
    vmem = pl.BlockSpec(memory_space=pltpu.VMEM)
    piece = (nb, rows, orbitals)
    fields, propagated = pl.pallas_call(
        functools.partial(kernel, (na, nb, nh, rows, electrons)),
        out_shape=(
            jax.ShapeDtypeStruct((walker_count, vectors), f32),
            jax.ShapeDtypeStruct((rows, nb * electrons), bf16),
        ),
        in_specs=[pl.BlockSpec(memory_space=pltpu.HBM)] * 5,
        out_specs=(vmem, vmem),
        scratch_shapes=[
            pltpu.VMEM(walkers.shape, bf16),
            pltpu.VMEM((electrons, walker_count, electrons), bf16),
            pltpu.VMEM((electrons * rows, vectors), bf16),
            pltpu.VMEM((depth, orbitals), bf16),
            pltpu.VMEM((walker_count, vectors), f32),
            pltpu.VMEM((walker_count, ceil_to(electrons, 16), electrons), bf16),
            pltpu.VMEM((walker_count, rows, electrons), bf16),
            pltpu.VMEM((walker_count * rows, electrons * rows), bf16),
            pltpu.VMEM((walker_count, vectors), f32),
            pltpu.VMEM((nb, rows, wide_electrons), bf16),
            pltpu.VMEM((vectors, depth), bf16),
            pltpu.VMEM((orbitals, orbitals), bf16),
            pltpu.VMEM((walker_count, depth), f32),
            pltpu.VMEM((2, nb * rows, depth), bf16),
            pltpu.VMEM((na, 8, LANES), f32),
            pltpu.VMEM((nb, 8, LANES), f32),
            pltpu.VMEM((walker_count, vectors), f32),
            pltpu.VMEM((nb, rows, wide_electrons), bf16),
            pltpu.VMEM((ORDER, padded, orbitals), bf16),
            pltpu.VMEM(piece, bf16),
            pltpu.VMEM(piece, bf16),
            pltpu.VMEM(piece, bf16),
            pltpu.VMEM((half, rows, orbitals), f32),
            pltpu.VMEM((half, rows, orbitals), f32),
            pltpu.VMEM(piece, bf16),
            pltpu.VMEM((half, rows, orbitals), bf16),
            pltpu.VMEM((half, rows, orbitals), bf16),
            pltpu.VMEM(piece, bf16),
            pltpu.VMEM(piece, bf16),
            pltpu.VMEM(piece, bf16),
            pltpu.VMEM((nb * rows, orbitals), bf16),
            pltpu.VMEM((nb, rows, wide_electrons), bf16),
            pltpu.VMEM((nb, rows, wide_electrons), bf16),
            dma((5,)),
            dma((3,)),
            dma((3,)),
            dma((2,)),
            dma((ORDER,)),
            dma((ORDER, PARTS)),
            dma((2,)),
            dma((2, 4)),
            dma,
            dma,
            dma,
            dma,
            dma,
            dma((4,)),
            dma((2,)),
        ],
        compiler_params=pltpu.CompilerParams(
            collective_id=0, has_side_effects=True, vmem_limit_bytes=48 * 1024 * 1024
        ),
    )(
        *(
            pltpu.with_memory_space_constraint(array, pltpu.HBM)
            for array in (
                walkers,
                jnp.transpose(inv_intersection, (1, 0, 2)),
                jnp.transpose(rotated, (2, 1, 0)).reshape(electrons * rows, vectors),
                cholesky.reshape(depth, orbitals),
                field_noise,
            )
        )
    )
    return fields, propagated


def solution(mesh):
    nh = mesh.shape["vec"]
    nb = 8 if mesh.shape["rows"] == 64 else 2
    na = mesh.shape["rows"] // nb
    placed = (P("rows", None), P(), P("vec", "rows", None), P("vec", "rows", None), P(None, "vec"))
    return jax.shard_map(
        functools.partial(local, na, nb, nh),
        mesh=mesh,
        in_specs=placed,
        out_specs=(P(None, "vec"), P("rows", "vec")),
        check_vma=False,
    )
```

```python
import functools

import jax
import jax.numpy as jnp
from jax import lax
from jax.experimental import pallas as pl
from jax.experimental.pallas import tpu as pltpu
from jax.sharding import PartitionSpec as P

MESH = pl.DeviceIdType.MESH
ORDER = 4
LANES = 128
TILE = 256
PARTS = 5

time_root = 0.1


def ceil_to(value, unit):
    return -(-value // unit) * unit


def place(nb, r):
    if nb == 2:
        return r % 2, r // 2
    x, y, low = r // 16, (r // 4) % 4, r % 4
    return ((y + y // 2) % 2) * 4 + low, x * 2 + y // 2


def device(nb, a, b):
    if nb == 2:
        return b * 2 + a
    x, half = b // 2, b % 2
    return x * 16 + (2 * half + (a // 4 + half) % 2) * 4 + a % 4


def kernel(
    dims,
    walkers_hbm,
    inverse_hbm,
    rotated_hbm,
    chol_hbm,
    noise_hbm,
    fields_ref,
    out_ref,
    walkers,
    inverse,
    rotated,
    chol,
    noise,
    by_walker,
    mixed,
    mixed_diag,
    part,
    phi,
    spread,
    order,
    wide,
    diag,
    fb_one,
    fb_two,
    phi_block,
    terms,
    send_far,
    send_right,
    send_left,
    hold_right,
    hold_left,
    own,
    far_left,
    far_right,
    op_own,
    op_early,
    op_late,
    turned_operator,
    result,
    landed,
    load_sem,
    fb_send,
    fb_recv,
    phi_sem,
    term_send,
    term_recv,
    far_send,
    far_recv,
    early_send,
    early_recv,
    own_send,
    own_recv,
    late_send,
    late_recv,
    out_sem,
):
    na, nb, nh, rows, electrons = dims
    half = nb // 2
    block = nb * rows
    depth = chol.shape[0]
    orbitals = chol.shape[1]
    padded = terms.shape[1]
    r = lax.axis_index("rows")
    h = lax.axis_index("vec")
    a, b = place(nb, r)

    def a_at(i):
        return sum(((a // bit) % 2 if not (na - i) // bit % 2 else 1 - (a // bit) % 2) * bit for bit in (4, 2, 1) if bit < na)

    def b_at(i):
        if nb == 2:
            return 1 - b
        step, turn = ((2, 1), (1, 1), (3, 1), (2, 0), (1, 0), (3, 0), (0, 1))[i - 1]
        return (b // 2 + step) % 4 * 2 + (1 - b % 2 if turn else b % 2)

    def a_peer(i):
        return (device(nb, a_at(i), b), h)

    def b_peer(i):
        return (device(nb, a, b_at(i)), h)

    def h_peer(i):
        return (r, (h + i) % nh)

    def send(src, dst, send_sem, recv_sem, peer):
        copy = pltpu.make_async_remote_copy(
            src_ref=src, dst_ref=dst, send_sem=send_sem, recv_sem=recv_sem, device_id=peer, device_id_type=MESH
        )
        copy.start()

    def wait(span, sem):
        pltpu.make_async_copy(span, span, sem).wait()

    pairs = ((walkers_hbm, walkers), (inverse_hbm, inverse), (rotated_hbm, rotated), (chol_hbm, chol), (noise_hbm, noise))
    loads = [pltpu.make_async_copy(src, dst, load_sem.at[i]) for i, (src, dst) in enumerate(pairs)]
    for i in (1, 0, 2):
        loads[i].start()

    barrier = pltpu.get_barrier_semaphore()
    def owner(j, step):
        return (device(nb, a, j), (h + step) % nh)

    peers = [a_peer(i) for i in range(1, na)] + [b_peer(i) for i in range(1, nb)]
    peers += [owner(j, step) for j in range(nb) for step in (1, nh - 1)]
    for peer in peers:
        pl.semaphore_signal(barrier, inc=1, device_id=peer, device_id_type=MESH)
    def fill(k, _):
        row = lax.broadcasted_iota(jnp.int32, (spread.shape[0], TILE), 0)
        lane = lax.broadcasted_iota(jnp.int32, (spread.shape[0], TILE), 1)
        here = row == (TILE // rows) * k + lane // rows
        spread[:, pl.ds(pl.multiple_of(k * TILE, TILE), TILE)] = jnp.where(here, 1.0, 0.0).astype(jnp.bfloat16)
        return 0

    lax.fori_loop(0, depth // TILE, fill, 0)

    count = mixed.shape[0]
    span = electrons * rows
    to = lax.broadcasted_iota(jnp.int32, (8 * count, 8 * count), 0)
    source = lax.broadcasted_iota(jnp.int32, (8 * count, 8 * count), 1)
    gather = jnp.where(source == (to % 8) * count + to // 8, 1.0, 0.0).astype(jnp.bfloat16)
    loads[1].wait()

    def eight(f):
        size = min(8, electrons - f)
        if size <= 0:
            return jnp.zeros((count, 8, electrons), jnp.float32)
        taken = inverse[f : f + size].reshape(size * count, electrons)
        return jnp.dot(gather[:, : size * count], taken, preferred_element_type=jnp.float32).reshape(count, 8, electrons)

    for f in range(0, electrons, 16):
        by_walker[:, f : f + 16, :] = jnp.concatenate([eight(f), eight(f + 8)], axis=1).astype(jnp.bfloat16)
    loads[0].wait()
    for w in range(count):
        mixed[w] = jnp.dot(
            walkers[:, w * electrons : (w + 1) * electrons],
            by_walker[w, :electrons, :],
            preferred_element_type=jnp.float32,
        ).astype(jnp.bfloat16)
    for start in range(0, span, TILE):
        here = pl.ds(start, min(TILE, span - start))
        spaced = jnp.dot(
            mixed[...].reshape(count * rows, electrons), spread[:electrons, here], preferred_element_type=jnp.float32
        )
        p = lax.broadcasted_iota(jnp.int32, spaced.shape, 0) % rows
        lane = lax.broadcasted_iota(jnp.int32, spaced.shape, 1) % rows
        mixed_diag[:, here] = jnp.where(p == lane, spaced, 0.0).astype(jnp.bfloat16)
    loads[3].start()
    loads[4].start()
    loads[2].wait()
    by_row = jnp.dot(mixed_diag[...], rotated[...], preferred_element_type=jnp.float32)
    part[...] = jnp.sum(by_row.reshape(count, rows, by_row.shape[1]), axis=1)

    pl.semaphore_wait(barrier, len(peers))

    fb_one[a] = part[...].astype(jnp.bfloat16)
    for i in range(1, na):
        send(fb_one.at[a], fb_one.at[a], fb_send.at[0], fb_recv.at[0], a_peer(i))

    phi[:, :, LANES:] = jnp.zeros((nb, rows, phi.shape[2] - LANES), jnp.bfloat16)
    for k in range(nh):

        @pl.when(h == k)
        def _():
            for j in range(nb):
                start = (k * nb + j) * electrons
                phi[j, :, :electrons] = walkers[:, start : start + electrons]

    for i in range(1, nb):
        send(phi.at[b_at(i)], phi_block.at[b], phi_sem.at[0], phi_sem.at[1], b_peer(i))
    phi_block[b] = phi[b]

    def arrange(k, _):
        lane = lax.broadcasted_iota(jnp.int32, (1, block), 1)
        source = device(nb, k, lane // rows) * rows + lane % rows
        row = lax.broadcasted_iota(jnp.int32, (orbitals, block), 0)
        here = pl.ds(pl.multiple_of(k * block, block), block)
        order[:, here] = jnp.where(row == source, 1.0, 0.0).astype(jnp.bfloat16)
        return 0

    lax.fori_loop(0, na, arrange, 0)

    wait(fb_one.at[pl.ds(0, na - 1)], fb_recv.at[0])
    total = fb_one[0].astype(jnp.float32)
    for i in range(1, na):
        total = total + fb_one[i].astype(jnp.float32)
    fb_two[b] = total.astype(jnp.bfloat16)
    for i in range(1, nb):
        send(fb_two.at[b], fb_two.at[b], fb_send.at[1], fb_recv.at[1], b_peer(i))

    wait(phi_block.at[pl.ds(0, nb - 1)], phi_sem.at[1])
    mine = pl.ds(pl.multiple_of(a * block, block), block)
    turned = jnp.transpose(phi_block[...].reshape(block, phi_block.shape[2]).astype(jnp.float32))
    first = turned[:padded, :]
    terms[0, :, mine] = first.astype(jnp.bfloat16)

    def some(c):
        return pl.ds(c * (padded // PARTS), padded // PARTS)

    def share(k, c):
        there = terms.at[k, some(c), mine]
        for i in range(1, na):
            send(there, there, term_send.at[k], term_recv.at[k, c], a_peer(i))

    for c in range(PARTS):
        share(0, c)

    wait(fb_two.at[pl.ds(0, nb - 1)], fb_recv.at[1])
    force_bias = fb_two[0].astype(jnp.float32)
    for i in range(1, nb):
        force_bias = force_bias + fb_two[i].astype(jnp.float32)
    loads[4].wait()
    fields = noise[...] - time_root * force_bias
    fields_ref[...] = fields
    scaled = (-time_root * fields).astype(jnp.bfloat16)

    wide[...] = jnp.dot(scaled, spread[...], preferred_element_type=jnp.float32)
    loads[3].wait()

    lower, upper = pl.ds(0, half), pl.ds(half, half)
    width = min(TILE, orbitals)
    tiles = orbitals // width

    def build(slot, c):
        p = lax.broadcasted_iota(jnp.int32, (rows, depth), 0)
        lane = lax.broadcasted_iota(jnp.int32, (rows, depth), 1)
        for w in range(nb):
            row = jnp.broadcast_to(wide[pl.ds(c * nb + w, 1), :], (rows, depth))
            diag[slot, w * rows : (w + 1) * rows, :] = jnp.where(p == lane % rows, row, 0.0).astype(jnp.bfloat16)

    def multiply(slot, store, some_spots):
        for here in some_spots:
            product = jnp.dot(diag[slot], chol[:, here], preferred_element_type=jnp.float32)
            store(here, product.reshape(nb, rows, width))

    def store_far(here, value):
        send_far[:, :, here] = value.astype(jnp.bfloat16)

    def store_right(here, value):
        hold_right[:, :, here] = value[:half]
        send_right[half:, :, here] = value[half:].astype(jnp.bfloat16)

    def store_left(here, value):
        send_left[:half, :, here] = value[:half].astype(jnp.bfloat16)
        hold_left[:, :, here] = value[half:]

    def store_own(here, value):
        own[:, :, here] = value.astype(jnp.bfloat16)

    spots = [pl.ds(n * width, width) for n in range(tiles)]
    right, left = h_peer(1), h_peer(nh - 1)
    build(0, (h + 2) % nh)
    for n, here in enumerate(spots):
        if n < 2:
            multiply(0, store_far, spots[:1] if n == 0 else spots[1:])
        send(send_far.at[lower, :, here], far_left.at[:, :, here], far_send.at[0], far_recv.at[0, n], right)
        send(send_far.at[upper, :, here], far_right.at[:, :, here], far_send.at[1], far_recv.at[1, n], left)
    build(1, (h + 1) % nh)
    build(0, (h + nh - 1) % nh)
    multiply(1, store_right, spots)
    build(1, h)
    multiply(0, store_left, spots)
    multiply(1, store_own, spots)
    for j in range(half):
        k = half + j
        send(send_right.at[k], op_early.at[b], early_send, early_recv, owner(k, 1))
        send(send_left.at[j], op_early.at[b], early_send, early_recv, owner(j, nh - 1))
    for i in range(1, nb):
        send(own.at[b_at(i)], op_own.at[b], own_send, own_recv, b_peer(i))
    op_own[b] = own[b]

    for n, here in enumerate(spots):
        wait(far_left.at[:, :, here], far_recv.at[0, n])
        send_right[:half, :, here] = (hold_right[:, :, here] + far_left[:, :, here].astype(jnp.float32)).astype(
            jnp.bfloat16
        )
        for j in range(half):
            send(send_right.at[j, :, here], op_late.at[b, :, here], late_send, late_recv.at[n], owner(j, 1))
        wait(far_right.at[:, :, here], far_recv.at[1, n])
        send_left[half:, :, here] = (hold_left[:, :, here] + far_right[:, :, here].astype(jnp.float32)).astype(
            jnp.bfloat16
        )
        for k in range(half, nb):
            send(send_left.at[k, :, here], op_late.at[b, :, here], late_send, late_recv.at[n], owner(k, nh - 1))

    wait(op_own.at[pl.ds(0, nb - 1)], own_recv)
    wait(op_early, early_recv)
    turned = jnp.zeros((block, orbitals), jnp.float32)
    for n, here in enumerate(spots):
        wait(op_late.at[:, :, here], late_recv.at[n])
        value = op_own[:, :, here].astype(jnp.float32) + op_early[:, :, here].astype(jnp.float32)
        value = (value + op_late[:, :, here].astype(jnp.float32)).astype(jnp.bfloat16)
        turned = turned + jnp.dot(value.reshape(block, width), order[here, :], preferred_element_type=jnp.float32)
    turned_operator[...] = turned.astype(jnp.bfloat16)

    summed = [first[c * (padded // PARTS) : (c + 1) * (padded // PARTS)] for c in range(PARTS)]
    for degree in range(1, ORDER + 1):
        for c in range(PARTS):
            wait(terms.at[degree - 1, some(c), pl.ds(0, (na - 1) * block)], term_recv.at[degree - 1, c])
            product = lax.dot_general(
                terms[degree - 1, some(c), :],
                turned_operator[...],
                (((1,), (1,)), ((), ())),
                preferred_element_type=jnp.float32,
            )
            term = (product / degree).astype(jnp.bfloat16)
            if degree < ORDER:
                terms[degree, some(c), mine] = term
                share(degree, c)
            summed[c] = summed[c] + term.astype(jnp.float32)

    tall = jnp.concatenate([*summed, jnp.zeros((result.shape[2] - padded, block), jnp.float32)], axis=0)
    result[...] = jnp.transpose(tall).astype(jnp.bfloat16).reshape(result.shape)
    for i in range(1, nb):
        send(result.at[b_at(i)], landed.at[b], out_sem.at[0], out_sem.at[1], b_peer(i))
    landed[b] = result[b]
    wait(landed.at[pl.ds(0, nb - 1)], out_sem.at[1])
    for j in range(nb):
        out_ref[:, j * electrons : (j + 1) * electrons] = landed[j, :, :electrons]

    wait(fb_one.at[pl.ds(0, na - 1)], fb_send.at[0])
    wait(fb_two.at[pl.ds(0, nb - 1)], fb_send.at[1])
    wait(phi.at[pl.ds(0, nb - 1)], phi_sem.at[0])
    for k in range(ORDER):
        wait(terms.at[k, :, pl.ds(0, (na - 1) * block)], term_send.at[k])
    wait(far_left, far_send.at[0])
    wait(far_right, far_send.at[1])
    wait(op_early, early_send)
    wait(op_late, late_send)
    wait(op_own.at[pl.ds(0, nb - 1)], own_send)
    wait(result.at[pl.ds(0, nb - 1)], out_sem.at[0])


def local(na, nb, nh, walkers, inv_intersection, rotated, cholesky, field_noise):
    walker_count, electrons = inv_intersection.shape[:2]
    rows = walkers.shape[0]
    vectors, _, orbitals = cholesky.shape
    wide_electrons = ceil_to(electrons, LANES)
    padded = ceil_to(electrons, 16)
    half = nb // 2
    bf16, f32 = jnp.bfloat16, jnp.float32
    depth = vectors * rows
    dma = pltpu.SemaphoreType.DMA
    vmem = pl.BlockSpec(memory_space=pltpu.VMEM)
    piece = (nb, rows, orbitals)
    fields, propagated = pl.pallas_call(
        functools.partial(kernel, (na, nb, nh, rows, electrons)),
        out_shape=(
            jax.ShapeDtypeStruct((walker_count, vectors), f32),
            jax.ShapeDtypeStruct((rows, nb * electrons), bf16),
        ),
        in_specs=[pl.BlockSpec(memory_space=pltpu.HBM)] * 5,
        out_specs=(vmem, vmem),
        scratch_shapes=[
            pltpu.VMEM(walkers.shape, bf16),
            pltpu.VMEM((electrons, walker_count, electrons), bf16),
            pltpu.VMEM((electrons * rows, vectors), bf16),
            pltpu.VMEM((depth, orbitals), bf16),
            pltpu.VMEM((walker_count, vectors), f32),
            pltpu.VMEM((walker_count, ceil_to(electrons, 16), electrons), bf16),
            pltpu.VMEM((walker_count, rows, electrons), bf16),
            pltpu.VMEM((walker_count * rows, electrons * rows), bf16),
            pltpu.VMEM((walker_count, vectors), f32),
            pltpu.VMEM((nb, rows, wide_electrons), bf16),
            pltpu.VMEM((vectors, depth), bf16),
            pltpu.VMEM((orbitals, orbitals), bf16),
            pltpu.VMEM((walker_count, depth), f32),
            pltpu.VMEM((2, nb * rows, depth), bf16),
            pltpu.VMEM((na, walker_count, vectors), bf16),
            pltpu.VMEM((nb, walker_count, vectors), bf16),
            pltpu.VMEM((nb, rows, wide_electrons), bf16),
            pltpu.VMEM((ORDER, padded, orbitals), bf16),
            pltpu.VMEM(piece, bf16),
            pltpu.VMEM(piece, bf16),
            pltpu.VMEM(piece, bf16),
            pltpu.VMEM((half, rows, orbitals), f32),
            pltpu.VMEM((half, rows, orbitals), f32),
            pltpu.VMEM(piece, bf16),
            pltpu.VMEM((half, rows, orbitals), bf16),
            pltpu.VMEM((half, rows, orbitals), bf16),
            pltpu.VMEM(piece, bf16),
            pltpu.VMEM(piece, bf16),
            pltpu.VMEM(piece, bf16),
            pltpu.VMEM((nb * rows, orbitals), bf16),
            pltpu.VMEM((nb, rows, wide_electrons), bf16),
            pltpu.VMEM((nb, rows, wide_electrons), bf16),
            dma((5,)),
            dma((2,)),
            dma((2,)),
            dma((2,)),
            dma((ORDER,)),
            dma((ORDER, PARTS)),
            dma((2,)),
            dma((2, 4)),
            dma,
            dma,
            dma,
            dma,
            dma,
            dma((4,)),
            dma((2,)),
        ],
        compiler_params=pltpu.CompilerParams(
            collective_id=0, has_side_effects=True, vmem_limit_bytes=48 * 1024 * 1024
        ),
    )(
        *(
            pltpu.with_memory_space_constraint(array, pltpu.HBM)
            for array in (
                walkers,
                jnp.transpose(inv_intersection, (1, 0, 2)),
                jnp.transpose(rotated, (2, 1, 0)).reshape(electrons * rows, vectors),
                cholesky.reshape(depth, orbitals),
                field_noise,
            )
        )
    )
    return fields, propagated


def solution(mesh):
    nh = mesh.shape["vec"]
    nb = 8 if mesh.shape["rows"] == 64 else 2
    na = mesh.shape["rows"] // nb
    placed = (P("rows", None), P(), P("vec", "rows", None), P("vec", "rows", None), P(None, "vec"))
    return jax.shard_map(
        functools.partial(local, na, nb, nh),
        mesh=mesh,
        in_specs=placed,
        out_specs=(P(None, "vec"), P("rows", "vec")),
        check_vma=False,
    )
```

```python
import functools

import jax
import jax.numpy as jnp
from jax import lax
from jax.experimental import pallas as pl
from jax.experimental.pallas import tpu as pltpu
from jax.sharding import PartitionSpec as P

MESH = pl.DeviceIdType.MESH
ORDER = 4
LANES = 128
TILE = 256
PARTS = 5

time_root = 0.1


def ceil_to(value, unit):
    return -(-value // unit) * unit


def place(nb, r):
    if nb == 2:
        return r % 2, r // 2
    x, y, low = r // 16, (r // 4) % 4, r % 4
    return ((y + y // 2) % 2) * 4 + low, x * 2 + y // 2


def device(nb, a, b):
    if nb == 2:
        return b * 2 + a
    x, half = b // 2, b % 2
    return x * 16 + (2 * half + (a // 4 + half) % 2) * 4 + a % 4


def kernel(
    dims,
    walkers_hbm,
    inverse_hbm,
    rotated_hbm,
    chol_hbm,
    noise_hbm,
    fields_ref,
    out_ref,
    walkers,
    inverse,
    rotated,
    chol,
    noise,
    by_walker,
    mixed,
    mixed_diag,
    part,
    phi,
    spread,
    order,
    wide,
    diag,
    fb_one,
    fb_two,
    phi_block,
    terms,
    send_far,
    send_right,
    send_left,
    hold_right,
    hold_left,
    own,
    far_left,
    far_right,
    op_own,
    op_early,
    op_late,
    turned_operator,
    result,
    landed,
    load_sem,
    fb_send,
    fb_recv,
    phi_sem,
    term_send,
    term_recv,
    far_send,
    far_recv,
    early_send,
    early_recv,
    own_send,
    own_recv,
    late_send,
    late_recv,
    out_sem,
):
    na, nb, nh, rows, electrons = dims
    half = nb // 2
    block = nb * rows
    depth = chol.shape[0]
    orbitals = chol.shape[1]
    padded = terms.shape[1]
    r = lax.axis_index("rows")
    h = lax.axis_index("vec")
    a, b = place(nb, r)

    def a_at(i):
        return sum(((a // bit) % 2 if not (na - i) // bit % 2 else 1 - (a // bit) % 2) * bit for bit in (4, 2, 1) if bit < na)

    def b_at(i):
        if nb == 2:
            return 1 - b
        step, turn = ((2, 1), (1, 1), (3, 1), (2, 0), (1, 0), (3, 0), (0, 1))[i - 1]
        return (b // 2 + step) % 4 * 2 + (1 - b % 2 if turn else b % 2)

    def a_peer(i):
        return (device(nb, a_at(i), b), h)

    def b_peer(i):
        return (device(nb, a, b_at(i)), h)

    def h_peer(i):
        return (r, (h + i) % nh)

    def send(src, dst, send_sem, recv_sem, peer):
        copy = pltpu.make_async_remote_copy(
            src_ref=src, dst_ref=dst, send_sem=send_sem, recv_sem=recv_sem, device_id=peer, device_id_type=MESH
        )
        copy.start()

    def wait(span, sem):
        pltpu.make_async_copy(span, span, sem).wait()

    pairs = ((walkers_hbm, walkers), (inverse_hbm, inverse), (rotated_hbm, rotated), (chol_hbm, chol), (noise_hbm, noise))
    early_f = ceil_to(electrons // 2, 16)
    first_f, last_f = pl.ds(0, early_f), pl.ds(early_f, electrons - early_f)
    pairs = (
        (walkers_hbm, walkers),
        (inverse_hbm.at[first_f], inverse.at[first_f]),
        *pairs[2:],
        (inverse_hbm.at[last_f], inverse.at[last_f]),
    )
    loads = [pltpu.make_async_copy(src, dst, load_sem.at[i]) for i, (src, dst) in enumerate(pairs)]
    for i in (1, 5, 0, 2):
        loads[i].start()

    barrier = pltpu.get_barrier_semaphore()
    def owner(j, step):
        return (device(nb, a, j), (h + step) % nh)

    peers = [a_peer(i) for i in range(1, na)] + [b_peer(i) for i in range(1, nb)]
    peers += [owner(j, step) for j in range(nb) for step in (1, nh - 1)]
    for peer in peers:
        pl.semaphore_signal(barrier, inc=1, device_id=peer, device_id_type=MESH)
    def fill(k, _):
        row = lax.broadcasted_iota(jnp.int32, (spread.shape[0], TILE), 0)
        lane = lax.broadcasted_iota(jnp.int32, (spread.shape[0], TILE), 1)
        here = row == (TILE // rows) * k + lane // rows
        spread[:, pl.ds(pl.multiple_of(k * TILE, TILE), TILE)] = jnp.where(here, 1.0, 0.0).astype(jnp.bfloat16)
        return 0

    lax.fori_loop(0, depth // TILE, fill, 0)

    count = mixed.shape[0]
    span = electrons * rows
    to = lax.broadcasted_iota(jnp.int32, (8 * count, 8 * count), 0)
    source = lax.broadcasted_iota(jnp.int32, (8 * count, 8 * count), 1)
    gather = jnp.where(source == (to % 8) * count + to // 8, 1.0, 0.0).astype(jnp.bfloat16)
    loads[1].wait()

    def eight(f):
        size = min(8, electrons - f)
        if size <= 0:
            return jnp.zeros((count, 8, electrons), jnp.float32)
        taken = inverse[f : f + size].reshape(size * count, electrons)
        return jnp.dot(gather[:, : size * count], taken, preferred_element_type=jnp.float32).reshape(count, 8, electrons)

    for f in range(0, electrons, 16):
        if f == early_f:
            loads[5].wait()
        by_walker[:, f : f + 16, :] = jnp.concatenate([eight(f), eight(f + 8)], axis=1).astype(jnp.bfloat16)
    loads[0].wait()
    for w in range(count):
        mixed[w] = jnp.dot(
            walkers[:, w * electrons : (w + 1) * electrons],
            by_walker[w, :electrons, :],
            preferred_element_type=jnp.float32,
        ).astype(jnp.bfloat16)
    for start in range(0, span, TILE):
        here = pl.ds(start, min(TILE, span - start))
        spaced = jnp.dot(
            mixed[...].reshape(count * rows, electrons), spread[:electrons, here], preferred_element_type=jnp.float32
        )
        p = lax.broadcasted_iota(jnp.int32, spaced.shape, 0) % rows
        lane = lax.broadcasted_iota(jnp.int32, spaced.shape, 1) % rows
        mixed_diag[:, here] = jnp.where(p == lane, spaced, 0.0).astype(jnp.bfloat16)
    loads[3].start()
    loads[4].start()
    loads[2].wait()
    by_row = jnp.dot(mixed_diag[...], rotated[...], preferred_element_type=jnp.float32)
    part[...] = jnp.sum(by_row.reshape(count, rows, by_row.shape[1]), axis=1)

    pl.semaphore_wait(barrier, len(peers))

    fb_one[a] = part[...].astype(jnp.bfloat16)
    for i in range(1, na):
        send(fb_one.at[a], fb_one.at[a], fb_send.at[0], fb_recv.at[0], a_peer(i))

    phi[:, :, LANES:] = jnp.zeros((nb, rows, phi.shape[2] - LANES), jnp.bfloat16)
    for k in range(nh):

        @pl.when(h == k)
        def _():
            for j in range(nb):
                start = (k * nb + j) * electrons
                phi[j, :, :electrons] = walkers[:, start : start + electrons]

    for i in range(1, nb):
        send(phi.at[b_at(i)], phi_block.at[b], phi_sem.at[0], phi_sem.at[1], b_peer(i))
    phi_block[b] = phi[b]

    def arrange(k, _):
        lane = lax.broadcasted_iota(jnp.int32, (1, block), 1)
        source = device(nb, k, lane // rows) * rows + lane % rows
        row = lax.broadcasted_iota(jnp.int32, (orbitals, block), 0)
        here = pl.ds(pl.multiple_of(k * block, block), block)
        order[:, here] = jnp.where(row == source, 1.0, 0.0).astype(jnp.bfloat16)
        return 0

    lax.fori_loop(0, na, arrange, 0)

    wait(fb_one.at[pl.ds(0, na - 1)], fb_recv.at[0])
    total = fb_one[0].astype(jnp.float32)
    for i in range(1, na):
        total = total + fb_one[i].astype(jnp.float32)
    fb_two[b] = total.astype(jnp.bfloat16)
    for i in range(1, nb):
        send(fb_two.at[b], fb_two.at[b], fb_send.at[1], fb_recv.at[1], b_peer(i))

    wait(phi_block.at[pl.ds(0, nb - 1)], phi_sem.at[1])
    mine = pl.ds(pl.multiple_of(a * block, block), block)
    turned = jnp.transpose(phi_block[...].reshape(block, phi_block.shape[2]).astype(jnp.float32))
    first = turned[:padded, :]
    terms[0, :, mine] = first.astype(jnp.bfloat16)

    def some(c):
        return pl.ds(c * (padded // PARTS), padded // PARTS)

    def share(k, c):
        there = terms.at[k, some(c), mine]
        for i in range(1, na):
            send(there, there, term_send.at[k], term_recv.at[k, c], a_peer(i))

    for c in range(PARTS):
        share(0, c)

    wait(fb_two.at[pl.ds(0, nb - 1)], fb_recv.at[1])
    force_bias = fb_two[0].astype(jnp.float32)
    for i in range(1, nb):
        force_bias = force_bias + fb_two[i].astype(jnp.float32)
    loads[4].wait()
    fields = noise[...] - time_root * force_bias
    fields_ref[...] = fields
    scaled = (-time_root * fields).astype(jnp.bfloat16)

    wide[...] = jnp.dot(scaled, spread[...], preferred_element_type=jnp.float32)
    loads[3].wait()

    lower, upper = pl.ds(0, half), pl.ds(half, half)
    width = min(TILE, orbitals)
    tiles = orbitals // width

    def build(slot, c):
        p = lax.broadcasted_iota(jnp.int32, (rows, depth), 0)
        lane = lax.broadcasted_iota(jnp.int32, (rows, depth), 1)
        for w in range(nb):
            row = jnp.broadcast_to(wide[pl.ds(c * nb + w, 1), :], (rows, depth))
            diag[slot, w * rows : (w + 1) * rows, :] = jnp.where(p == lane % rows, row, 0.0).astype(jnp.bfloat16)

    def multiply(slot, store, some_spots):
        for here in some_spots:
            product = jnp.dot(diag[slot], chol[:, here], preferred_element_type=jnp.float32)
            store(here, product.reshape(nb, rows, width))

    def store_far(here, value):
        send_far[:, :, here] = value.astype(jnp.bfloat16)

    def store_right(here, value):
        hold_right[:, :, here] = value[:half]
        send_right[half:, :, here] = value[half:].astype(jnp.bfloat16)

    def store_left(here, value):
        send_left[:half, :, here] = value[:half].astype(jnp.bfloat16)
        hold_left[:, :, here] = value[half:]

    def store_own(here, value):
        own[:, :, here] = value.astype(jnp.bfloat16)

    spots = [pl.ds(n * width, width) for n in range(tiles)]
    right, left = h_peer(1), h_peer(nh - 1)
    build(0, (h + 2) % nh)
    for n, here in enumerate(spots):
        if n < 2:
            multiply(0, store_far, spots[:1] if n == 0 else spots[1:])
        send(send_far.at[lower, :, here], far_left.at[:, :, here], far_send.at[0], far_recv.at[0, n], right)
        send(send_far.at[upper, :, here], far_right.at[:, :, here], far_send.at[1], far_recv.at[1, n], left)
    build(1, h)
    multiply(1, store_own, spots)
    for i in range(1, nb):
        send(own.at[b_at(i)], op_own.at[b], own_send, own_recv, b_peer(i))
    op_own[b] = own[b]
    build(0, (h + 1) % nh)
    build(1, (h + nh - 1) % nh)
    multiply(0, store_right, spots)
    multiply(1, store_left, spots)

    for j in range(half):
        k = half + j
        send(send_right.at[k], op_early.at[b], early_send, early_recv, owner(k, 1))
        send(send_left.at[j], op_early.at[b], early_send, early_recv, owner(j, nh - 1))

    for n, here in enumerate(spots):
        wait(far_left.at[:, :, here], far_recv.at[0, n])
        send_right[:half, :, here] = (hold_right[:, :, here] + far_left[:, :, here].astype(jnp.float32)).astype(
            jnp.bfloat16
        )
        for j in range(half):
            send(send_right.at[j, :, here], op_late.at[b, :, here], late_send, late_recv.at[n], owner(j, 1))
        wait(far_right.at[:, :, here], far_recv.at[1, n])
        send_left[half:, :, here] = (hold_left[:, :, here] + far_right[:, :, here].astype(jnp.float32)).astype(
            jnp.bfloat16
        )
        for k in range(half, nb):
            send(send_left.at[k, :, here], op_late.at[b, :, here], late_send, late_recv.at[n], owner(k, nh - 1))

    wait(op_own.at[pl.ds(0, nb - 1)], own_recv)
    wait(op_early, early_recv)
    turned = jnp.zeros((block, orbitals), jnp.float32)
    for n, here in enumerate(spots):
        wait(op_late.at[:, :, here], late_recv.at[n])
        value = op_own[:, :, here].astype(jnp.float32) + op_early[:, :, here].astype(jnp.float32)
        value = (value + op_late[:, :, here].astype(jnp.float32)).astype(jnp.bfloat16)
        turned = turned + jnp.dot(value.reshape(block, width), order[here, :], preferred_element_type=jnp.float32)
    turned_operator[...] = turned.astype(jnp.bfloat16)

    summed = [first[c * (padded // PARTS) : (c + 1) * (padded // PARTS)] for c in range(PARTS)]
    for degree in range(1, ORDER + 1):
        for c in range(PARTS):
            wait(terms.at[degree - 1, some(c), pl.ds(0, (na - 1) * block)], term_recv.at[degree - 1, c])
            product = lax.dot_general(
                terms[degree - 1, some(c), :],
                turned_operator[...],
                (((1,), (1,)), ((), ())),
                preferred_element_type=jnp.float32,
            )
            term = (product / degree).astype(jnp.bfloat16)
            if degree < ORDER:
                terms[degree, some(c), mine] = term
                share(degree, c)
            summed[c] = summed[c] + term.astype(jnp.float32)

    tall = jnp.concatenate([*summed, jnp.zeros((result.shape[2] - padded, block), jnp.float32)], axis=0)
    result[...] = jnp.transpose(tall).astype(jnp.bfloat16).reshape(result.shape)
    for i in range(1, nb):
        send(result.at[b_at(i)], landed.at[b], out_sem.at[0], out_sem.at[1], b_peer(i))
    landed[b] = result[b]
    wait(landed.at[pl.ds(0, nb - 1)], out_sem.at[1])
    for j in range(nb):
        out_ref[:, j * electrons : (j + 1) * electrons] = landed[j, :, :electrons]

    wait(fb_one.at[pl.ds(0, na - 1)], fb_send.at[0])
    wait(fb_two.at[pl.ds(0, nb - 1)], fb_send.at[1])
    wait(phi.at[pl.ds(0, nb - 1)], phi_sem.at[0])
    for k in range(ORDER):
        wait(terms.at[k, :, pl.ds(0, (na - 1) * block)], term_send.at[k])
    wait(far_left, far_send.at[0])
    wait(far_right, far_send.at[1])
    wait(op_early, early_send)
    wait(op_late, late_send)
    wait(op_own.at[pl.ds(0, nb - 1)], own_send)
    wait(result.at[pl.ds(0, nb - 1)], out_sem.at[0])


def local(na, nb, nh, walkers, inv_intersection, rotated, cholesky, field_noise):
    walker_count, electrons = inv_intersection.shape[:2]
    rows = walkers.shape[0]
    vectors, _, orbitals = cholesky.shape
    wide_electrons = ceil_to(electrons, LANES)
    padded = ceil_to(electrons, 16)
    half = nb // 2
    bf16, f32 = jnp.bfloat16, jnp.float32
    depth = vectors * rows
    dma = pltpu.SemaphoreType.DMA
    vmem = pl.BlockSpec(memory_space=pltpu.VMEM)
    piece = (nb, rows, orbitals)
    fields, propagated = pl.pallas_call(
        functools.partial(kernel, (na, nb, nh, rows, electrons)),
        out_shape=(
            jax.ShapeDtypeStruct((walker_count, vectors), f32),
            jax.ShapeDtypeStruct((rows, nb * electrons), bf16),
        ),
        in_specs=[pl.BlockSpec(memory_space=pltpu.HBM)] * 5,
        out_specs=(vmem, vmem),
        scratch_shapes=[
            pltpu.VMEM(walkers.shape, bf16),
            pltpu.VMEM((electrons, walker_count, electrons), bf16),
            pltpu.VMEM((electrons * rows, vectors), bf16),
            pltpu.VMEM((depth, orbitals), bf16),
            pltpu.VMEM((walker_count, vectors), f32),
            pltpu.VMEM((walker_count, ceil_to(electrons, 16), electrons), bf16),
            pltpu.VMEM((walker_count, rows, electrons), bf16),
            pltpu.VMEM((walker_count * rows, electrons * rows), bf16),
            pltpu.VMEM((walker_count, vectors), f32),
            pltpu.VMEM((nb, rows, wide_electrons), bf16),
            pltpu.VMEM((vectors, depth), bf16),
            pltpu.VMEM((orbitals, orbitals), bf16),
            pltpu.VMEM((walker_count, depth), f32),
            pltpu.VMEM((2, nb * rows, depth), bf16),
            pltpu.VMEM((na, walker_count, vectors), bf16),
            pltpu.VMEM((nb, walker_count, vectors), bf16),
            pltpu.VMEM((nb, rows, wide_electrons), bf16),
            pltpu.VMEM((ORDER, padded, orbitals), bf16),
            pltpu.VMEM(piece, bf16),
            pltpu.VMEM(piece, bf16),
            pltpu.VMEM(piece, bf16),
            pltpu.VMEM((half, rows, orbitals), f32),
            pltpu.VMEM((half, rows, orbitals), f32),
            pltpu.VMEM(piece, bf16),
            pltpu.VMEM((half, rows, orbitals), bf16),
            pltpu.VMEM((half, rows, orbitals), bf16),
            pltpu.VMEM(piece, bf16),
            pltpu.VMEM(piece, bf16),
            pltpu.VMEM(piece, bf16),
            pltpu.VMEM((nb * rows, orbitals), bf16),
            pltpu.VMEM((nb, rows, wide_electrons), bf16),
            pltpu.VMEM((nb, rows, wide_electrons), bf16),
            dma((6,)),
            dma((2,)),
            dma((2,)),
            dma((2,)),
            dma((ORDER,)),
            dma((ORDER, PARTS)),
            dma((2,)),
            dma((2, 4)),
            dma,
            dma,
            dma,
            dma,
            dma,
            dma((4,)),
            dma((2,)),
        ],
        compiler_params=pltpu.CompilerParams(
            collective_id=0, has_side_effects=True, vmem_limit_bytes=48 * 1024 * 1024
        ),
    )(
        *(
            pltpu.with_memory_space_constraint(array, pltpu.HBM)
            for array in (
                walkers,
                jnp.transpose(inv_intersection, (1, 0, 2)),
                jnp.transpose(rotated, (2, 1, 0)).reshape(electrons * rows, vectors),
                cholesky.reshape(depth, orbitals),
                field_noise,
            )
        )
    )
    return fields, propagated


def solution(mesh):
    nh = mesh.shape["vec"]
    nb = 8 if mesh.shape["rows"] == 64 else 2
    na = mesh.shape["rows"] // nb
    placed = (P("rows", None), P(), P("vec", "rows", None), P("vec", "rows", None), P(None, "vec"))
    return jax.shard_map(
        functools.partial(local, na, nb, nh),
        mesh=mesh,
        in_specs=placed,
        out_specs=(P(None, "vec"), P("rows", "vec")),
        check_vma=False,
    )
```
